512 devices in a mesh: leaf: 512 (over y, z, x, core).
Axes of the slice: x: 4, y: 4, z: 16, core: 2. Of those that a mesh axis runs over, the one named last changes fastest.
Arguments:
- rhs: bfloat16 [4, 16384], P(None, 'leaf'), may hold values from -6 to 6
- x_sep: bfloat16 [16384, 29400], P('leaf'), may hold values from -2 to 2
- x_loc: bfloat16 [16384, 4096], P('leaf'), may hold values from -2 to 2
- sep_sizes: int32 [9], replicated, may hold values from 100 to 12800, as said below
Outputs:
- solution: float32 [4, 16384], P(None, 'leaf')
The draws below stay inside these ranges and needn't reach their ends.
Inputs may be any that keep to these rules, and one draw needn't show every extreme that they name: `sep_sizes`: entry l counts the active leading columns of level l, from half of its width 12800 // (4^(l // 3) * 2^(l % 3)), rounded down, to all of it; entry 0 is always complete and the last entry always holds exactly half of its width.
All inputs are finite; a program needn't handle non-finite values.
Results may differ from the reference program's by a relative error of at most 0.0004.
Values may be sent and summed in bfloat16 or wider, within the bound.
A program may use at most 64 MiB of HBM per device.

```python
import jax
import jax.numpy as jnp
from jax import lax

SEP_TOP = 12800
LOC = 4096
ROWS_DEV = 32
RHS = 4
LEV = 9
ROWS = 16384
COLS = 29400
N_LEAF = 512


def column_scales(levels):
    pieces = []
    for level_no in range(levels):
        block_width = SEP_TOP // (4 ** (level_no // 3) * 2 ** (level_no % 3))
        group_rows = ROWS_DEV * 2 ** (levels - level_no)
        level_scale = (block_width * group_rows * (levels + 1.0)) ** (-0.25)
        pieces.append(jnp.full((block_width,), level_scale, jnp.float32))
    return jnp.concatenate(pieces)


def draw_x_sep(key, part):
    key = jax.random.fold_in(key, 11)
    array_shape = (ROWS, COLS)
    values = jnp.clip(jax.random.normal(key, array_shape, jnp.float32), -5.0, 5.0)
    return (values * column_scales(LEV)).astype(jnp.bfloat16)


def draw_x_loc(key, part):
    key = jax.random.fold_in(key, 17)
    array_shape = (ROWS, LOC)
    local_scale = (LOC * ROWS_DEV * (LEV + 1.0)) ** (-0.25)
    values = jnp.clip(jax.random.normal(key, array_shape, jnp.float32), -5.0, 5.0)
    return (values * local_scale).astype(jnp.bfloat16)


def draw_sep_sizes(key, part):
    key = jax.random.fold_in(key, 13)
    widths = jnp.array([SEP_TOP // (4 ** (level_no // 3) * 2 ** (level_no % 3)) for level_no in range(LEV)], jnp.int32)
    size_key, full_key = jax.random.split(key)
    drawn = jax.random.randint(size_key, (LEV,), widths // 2, widths + 1)
    full_level = jax.random.randint(full_key, (), 0, LEV)
    level_ids = jnp.arange(LEV, dtype=jnp.int32)
    drawn = jnp.where(level_ids == full_level, widths, drawn)
    drawn = jnp.where(level_ids == 0, widths, drawn)
    drawn = jnp.where(level_ids == LEV - 1, widths // 2, drawn)
    return drawn.astype(jnp.int32)


def block_levels(stream_key, shape, cuts, low, high):
    gain, own = 1.0, jax.random.fold_in(stream_key, 6)
    for position, shards_of in cuts:
        draws = jnp.exp(jax.random.uniform(jax.random.fold_in(own, position), (shards_of,), jnp.float32, low / len(cuts), high / len(cuts)))
        gain = gain * jnp.repeat(draws, shape[position] // shards_of).reshape([-1 if axis == position else 1 for axis in range(len(shape))])
    return gain


def centred(own_key, extent, scale, limit, cuts=(), kind=jnp.bfloat16):
    values = scale * jax.random.normal(own_key, extent, jnp.float32)
    if cuts:
        values = values * block_levels(own_key, extent, cuts, -0.22, 0.18)
    return jnp.clip(values, -limit, limit).astype(kind)


def setup_inputs(seed: int = 0) -> dict:
    keys = jax.random.split(jax.random.key(seed), 5)
    return {
        "rhs": centred(keys[0], (RHS, ROWS), 1.0, 6.0, ((1, 512),)),
        "x_sep": draw_x_sep(jax.random.fold_in(keys[4], 71), 0),
        "x_loc": draw_x_loc(jax.random.fold_in(keys[4], 71), 0),
        "sep_sizes": draw_sep_sizes(jax.random.fold_in(keys[4], 71), 0),
    }


def level_width(top, level_no):
    return top // (4 ** (level_no // 3) * 2 ** (level_no % 3))


def reference(rhs, x_sep, x_loc, sep_sizes):
    devices = N_LEAF
    rhs_dev = rhs.reshape(RHS, devices, ROWS_DEV).transpose(1, 0, 2)
    sep_dev = x_sep.reshape(devices, ROWS_DEV, COLS)
    loc_dev = x_loc.reshape(devices, ROWS_DEV, LOC)
    contrib = lax.map(lambda operands: jnp.dot(operands[0], operands[1], preferred_element_type=jnp.float32), (rhs_dev, sep_dev))
    coarse = []
    offset = 0
    for level_no in range(LEV):
        block_width = level_width(SEP_TOP, level_no)
        groups = 2 ** level_no
        summed = contrib[:, :, offset:offset + block_width].reshape(groups, devices // groups, RHS, block_width).sum(axis=1)
        active = jnp.arange(block_width, dtype=jnp.int32) < sep_sizes[level_no]
        coarse.append(jnp.where(active, summed, jnp.float32(0.0)).astype(jnp.bfloat16))
        offset = offset + block_width

    def one_device(packed):
        device_no, rhs_one, sep_one, loc_one = packed
        pieces = []
        for level_no in range(LEV):
            group_no = (device_no // (devices // 2 ** level_no)).astype(jnp.int32)
            pieces.append(lax.dynamic_index_in_dim(coarse[level_no], group_no, 0, keepdims=False))
        joined = jnp.concatenate(pieces, axis=1)
        interior = jnp.dot(rhs_one, loc_one, preferred_element_type=jnp.float32).astype(jnp.bfloat16)
        return jnp.dot(joined, sep_one.T, preferred_element_type=jnp.float32) + jnp.dot(interior, loc_one.T, preferred_element_type=jnp.float32)

    result = lax.map(one_device, (jnp.arange(devices, dtype=jnp.int32), rhs_dev, sep_dev, loc_dev))
    return result.transpose(1, 0, 2).reshape(RHS, devices * ROWS_DEV)
```

```python
import functools

import jax
import jax.numpy as jnp
from jax import lax
from jax.experimental import pallas as pl
from jax.experimental.pallas import tpu as pltpu
from jax.sharding import PartitionSpec as P

MESH = pl.DeviceIdType.MESH
F32, BF16 = jnp.float32, jnp.bfloat16

CORE, X0, X1, Z0, Z1, Z2, Z3, Y0, Y1 = (1 << b for b in range(9))

ZONES = ((0, 100), (100, 50), (150, 64), (214, 16))
WIDE = (13, 7, 8, 2)
AT = (0, 13, 20, 28)
BLOCKS = 30
COLS = 29400
ENDS = (12800, 19200, 22400, 25600, 27200, 28000, 28800, 29200, 29400)
STARTS = (0,) + ENDS[:-1]
LOC = 4096


def window(zone, i):
    first, tiles = ZONES[zone]
    return first + (tiles * i) // 8


def column_of(zone, core, j):
    shape = (16, 128)
    i = 4 * core + lax.broadcasted_iota(jnp.int32, shape, 0) // 4
    lane = lax.broadcasted_iota(jnp.int32, shape, 1)
    first, tiles = ZONES[zone]
    start = first + (tiles * i) // 8
    end = first + (tiles * (i + 1)) // 8
    return (start + j) * 128 + lane, end * 128


def hops(mask):
    x, y = (mask // X0) % 4, (mask // Y0) % 4
    return (x > 0) + (x == 2) + (y > 0) + (y == 2) + (mask // Z0) % 2


def masks_of(bits):
    found = [0]
    for bit in bits:
        found += [m | bit for m in found]
    return sorted(found[1:], key=hops, reverse=True)


PLANE = masks_of((X0, X1, Z0, Y0, Y1))
PAIR = masks_of((X0, X1, Z0, Y0))
LINE = masks_of((X0, X1, Z0))
DEPTH = [m * Z1 for m in (4, 5, 3, 6, 2, 7, 1)]


def kernel(rhs_hbm, sizes_hbm, xsep_ref, xloc_ref, out_ref,
           rhs_ref, sizes_ref, xs, tail, xl, mine, send_core, recv_core, recv_ab, recv_c, recv_d, part_ab, part_c, deep_ab, deep_c, full,
           small_sem, load_sem, loc_sem, core_send, core_recv, rs_send, rs_recv, z_send, z_recv, ag_send, ag_recv,
           relay_send, relay_recv):
    me = lax.axis_index("leaf")

    def bit(b):
        return (me // b) % 2

    core = bit(CORE)
    y0, y1 = bit(Y0), bit(Y1)
    k = 2 * ((me // X0) % 4) + bit(Z0)
    delta = {b: (1 - 2 * bit(b)) * b for b in (CORE, X0, X1, Z0, Z1, Z2, Z3, Y0, Y1)}

    def partner(mask):
        other = me
        for b, d in delta.items():
            if mask & b:
                other = other + d
        return other

    def remote(src, dst, send, recv, device):
        return pltpu.make_async_remote_copy(
            src_ref=src, dst_ref=dst, send_sem=send, recv_sem=recv, device_id=(device,), device_id_type=MESH
        )

    def drain(ref, sem):
        pltpu.make_async_copy(ref, ref, sem).wait()

    rhs_copy = pltpu.make_async_copy(rhs_hbm, rhs_ref, small_sem.at[0])
    sizes_copy = pltpu.make_async_copy(sizes_hbm, sizes_ref, small_sem.at[1])
    rhs_copy.start()
    sizes_copy.start()

    loads = {}
    for zone in range(4):
        for half in (1, 0):
            owner = core if half == 0 else 1 - core
            group = []
            for s in range(4):
                begin0, begin1 = window(zone, s), window(zone, 4 + s)
                width = WIDE[zone] * 128
                at = AT[zone] * 128
                rows = pl.ds(32 * s, 32)
                sem = load_sem.at[half, zone, s]
                if zone == 3 and s == 3:
                    group.append((begin0, begin1, sem, rows, at, owner))
                    continue
                start = pl.multiple_of((begin0 + owner * (begin1 - begin0)) * 128, 128)
                copy = pltpu.make_async_copy(
                    xsep_ref.at[:, pl.ds(start, width)], xs.at[half, rows, pl.ds(at, width)], sem
                )
                copy.start()
                group.append(copy)
            loads[zone, half] = group

    def last_copies(half, last):
        begin0, begin1, sem, rows, at, owner = loads[3, half][3]
        if not last:
            return [pltpu.make_async_copy(
                xsep_ref.at[:, pl.ds(begin0 * 128, 256)], xs.at[half, rows, pl.ds(at, 256)], sem)]
        rest = COLS - (begin1 + 1) * 128
        return [
            pltpu.make_async_copy(
                xsep_ref.at[:, pl.ds(begin1 * 128, 128)], xs.at[half, rows, pl.ds(at, 128)], sem),
            pltpu.make_async_copy(
                xsep_ref.at[:, pl.ds((begin1 + 1) * 128, rest)], tail, load_sem.at[half, 3, 4]),
        ]

    def last_do(action):
        for half in (0, 1):
            owner = core if half == 0 else 1 - core
            for last in (False, True):
                @pl.when(owner == int(last))
                def _():
                    for copy in last_copies(half, last):
                        action(copy)

    last_do(lambda copy: copy.start())
    loc_copies = [
        pltpu.make_async_copy(xloc_ref.at[:, pl.ds(1024 * s, 1024)], xl.at[pl.ds(32 * s, 32), :], loc_sem.at[s])
        for s in range(4)
    ]
    for copy in loc_copies:
        copy.start()

    barrier = pltpu.get_barrier_semaphore()
    greeted = DEPTH + PLANE + [CORE]
    for mask in greeted:
        pl.semaphore_signal(barrier, inc=1, device_id=(partner(mask),), device_id_type=MESH)

    row = lax.broadcasted_iota(jnp.int32, (16, 128), 0)
    lane = lax.broadcasted_iota(jnp.int32, (16, 128), 1)
    diagonal = row // 4 == lane // 32
    pick_rows = (lax.broadcasted_iota(jnp.int32, (16, 4), 0) % 4 == lax.broadcasted_iota(jnp.int32, (16, 4), 1))
    pick_lanes = (lax.broadcasted_iota(jnp.int32, (32, 128), 1) % 32 == lax.broadcasted_iota(jnp.int32, (32, 128), 0))
    rhs_copy.wait()
    sizes_copy.wait()
    tall = jnp.dot(pick_rows.astype(BF16), rhs_ref[...], preferred_element_type=F32).astype(BF16)
    wide = jnp.dot(tall, pick_lanes.astype(BF16), preferred_element_type=F32)
    rhs16 = jnp.where(diagonal, wide, 0.0).astype(BF16)

    def contributions(zone, half, store):
        columns = pl.ds(AT[zone] * 128, WIDE[zone] * 128)
        product = jnp.dot(rhs16, xs[half, :, columns], preferred_element_type=F32)
        for j in range(WIDE[zone]):
            store[AT[zone] + j] = product[:, 128 * j : 128 * j + 128]

    def place_tail(half):
        @pl.when((core if half == 0 else 1 - core) == 1)
        def _():
            rest = jnp.concatenate([tail[...], jnp.zeros((32, 128 - tail.shape[1]), BF16)], axis=1)
            xs[half, 96:128, BLOCKS * 128 - 128 : BLOCKS * 128] = rest

    for zone in range(4):
        for half in (1, 0):
            for copy in loads[zone, half]:
                if not isinstance(copy, tuple):
                    copy.wait()
        if zone == 3:
            last_do(lambda copy: copy.wait())
            place_tail(1)
            place_tail(0)
        contributions(zone, 1, send_core)
        contributions(zone, 0, mine)

    pl.semaphore_wait(barrier, len(greeted))

    sibling = partner(CORE)
    core_copies = []
    for zone in range(4):
        blocks = pl.ds(AT[zone], WIDE[zone])
        copy = remote(send_core.at[blocks], recv_core.at[blocks], core_send.at[zone], core_recv.at[zone], sibling)
        copy.start()
        core_copies.append(copy)

    base = me - me % Z1 + core - y1 * Y1 - y0 * Y0

    def place(kk):
        return (kk // 2) * X0 + (kk % 2) * Z0

    def owner_a(a):
        return base + (a % 2) * Y1 + core * Y0 + place(a // 2)

    def owner_b(b):
        return base + y1 * Y1 + (1 - core) * Y0 + place(b)

    def owner_c(d):
        return base + y1 * Y1 + y0 * Y0 + place(d)

    role_a = y0 == core
    a_mine = 2 * k + y1
    owns_a = jnp.logical_and(role_a, a_mine < WIDE[0])
    owns_b = jnp.logical_and(jnp.logical_not(role_a), k < WIDE[1])
    slot_a = 16 * y1 + 8 * y0 + k
    slot_b = 8 * y0 + k

    def scatter(zone, count, owner, slot, landing, sem):
        for j in range(count):
            block = AT[zone] + j
            to = owner(j)

            @pl.when(to == me)
            def _():
                landing[slot] = mine[block]

            @pl.when(to != me)
            def _():
                remote(mine.at[block], landing.at[slot], rs_send.at[sem], rs_recv.at[sem], to).start()

    for zone in range(4):
        core_copies[zone].wait_recv()
        for j in range(WIDE[zone]):
            block = AT[zone] + j
            mine[block] = mine[block] + recv_core[block]
        if zone == 0:
            scatter(0, WIDE[0], owner_a, slot_a, recv_ab, 0)
        elif zone == 1:
            scatter(1, WIDE[1], owner_b, slot_b, recv_ab, 1)
        elif zone == 2:
            scatter(2, WIDE[2], owner_c, k, recv_c, 2)

    def d_copy(n, mask):
        return remote(mine.at[pl.ds(AT[3], 2)], recv_d.at[n], rs_send.at[3 + n], rs_recv.at[3 + n], partner(mask))

    def d_do(action):
        for n, mask in enumerate(LINE):
            if mask & Z0:
                @pl.when(core == 0)
                def _():
                    action(d_copy(n, mask))
            else:
                action(d_copy(n, mask))

    d_do(lambda copy: copy.start())

    def total(landing, count):
        acc = [landing[i] for i in range(4)]
        for i in range(4, count):
            acc[i % 4] = acc[i % 4] + landing[i]
        return (acc[0] + acc[1]) + (acc[2] + acc[3])

    def deep_copies(src, landing, at):
        return [
            remote(src, landing.at[m // Z1 - 1], z_send.at[at], z_recv.at[at], partner(m)) for m in DEPTH
        ]

    @pl.when(owns_a)
    def _():
        drain(recv_ab.at[pl.ds(0, 31)], rs_recv.at[0])
        part_ab[...] = total(recv_ab, 32)

    @pl.when(owns_b)
    def _():
        drain(recv_ab.at[pl.ds(0, 15)], rs_recv.at[1])
        part_ab[...] = total(recv_ab, 16)

    owns_ab = jnp.logical_or(owns_a, owns_b)

    @pl.when(owns_ab)
    def _():
        for copy in deep_copies(part_ab, deep_ab, 0):
            copy.start()

    drain(recv_c.at[pl.ds(0, 7)], rs_recv.at[2])
    part_c[...] = total(recv_c, 8)
    deep_c_copies = deep_copies(part_c, deep_c, 1)
    for m, copy in zip(DEPTH, deep_c_copies):
        if m & Z3:
            @pl.when(core == 0)
            def _():
                copy.start()
        else:
            copy.start()

    def active(columns, zone):
        lo, hi = ZONES[zone][0] * 128, sum(ZONES[zone]) * 128
        keep = None
        for level in range(9):
            if STARTS[level] < hi and ENDS[level] > lo:
                limit = STARTS[level] + sizes_ref[level]
                inside = jnp.logical_and(
                    jnp.logical_and(columns >= STARTS[level], columns < ENDS[level]), columns < limit)
                keep = inside if keep is None else jnp.logical_or(keep, inside)
        return keep

    def rounded(values, columns, end, zone):
        keep = jnp.logical_and(active(columns, zone), columns < end)
        return jnp.where(keep, values, 0.0).astype(BF16)

    d_do(lambda copy: copy.wait_recv())
    for j in range(2):
        columns, end = column_of(3, core, j)
        value = mine[AT[3] + j]
        for n, mask in enumerate(LINE):
            if mask & Z0:
                bound = jnp.where(core == 0, ENDS[5], 0)
            else:
                bound = ENDS[6] if mask & X1 else ENDS[7]
            value = value + jnp.where(columns < bound, recv_d[n, j], 0.0)
        full[0, AT[3] + j] = rounded(value, columns, end, 3)

    def relay(zone, at):
        blocks = pl.ds(AT[zone], WIDE[zone])
        return remote(full.at[0, blocks], full.at[1, blocks], relay_send.at[at], relay_recv.at[at], sibling)

    relay(3, 3).start()

    for copy in loc_copies:
        copy.wait()
    interior = jnp.dot(rhs16, xl[...], preferred_element_type=F32).astype(BF16)
    contract = (((1,), (1,)), ((), ()))
    acc = lax.dot_general(interior, xl[...], contract, preferred_element_type=F32)

    def product(zone, half):
        blocks = jnp.concatenate([full[half, AT[zone] + j] for j in range(WIDE[zone])], axis=1)
        columns = pl.ds(AT[zone] * 128, WIDE[zone] * 128)
        return lax.dot_general(blocks, xs[half, :, columns], contract, preferred_element_type=F32)

    def deep_total(part, landing):
        value = part[...]
        for i in range(7):
            value = value + landing[i]
        return value

    def gather(block, masks, sem):
        for mask in masks:
            remote(full.at[0, block], full.at[0, block], ag_send.at[sem], ag_recv.at[sem], partner(mask)).start()

    @pl.when(owns_ab)
    def _():
        drain(deep_ab, z_recv.at[0])

    @pl.when(owns_a)
    def _():
        columns, end = column_of(0, core, a_mine)
        full[0, a_mine] = rounded(deep_total(part_ab, deep_ab), columns, end, 0)
        gather(a_mine, PLANE, 0)

    @pl.when(owns_b)
    def _():
        columns, end = column_of(1, core, k)
        full[0, AT[1] + k] = rounded(deep_total(part_ab, deep_ab), columns, end, 1)
        gather(AT[1] + k, PAIR, 1)

    @pl.when(core == 0)
    def _():
        drain(deep_c, z_recv.at[1])

    @pl.when(core == 1)
    def _():
        drain(deep_c.at[pl.ds(0, 3)], z_recv.at[1])

    columns, end = column_of(2, core, k)
    value = part_c[...]
    for m in range(1, 8):
        bound = ENDS[4] if m == 1 else ENDS[3] if m < 4 else jnp.where(core == 0, ENDS[2], 0)
        value = value + jnp.where(columns < bound, deep_c[m - 1], 0.0)
    full[0, AT[2] + k] = rounded(value, columns, end, 2)
    gather(AT[2] + k, LINE, 2)

    drain(full.at[0, pl.ds(AT[2], 7)], ag_recv.at[2])
    relay(2, 2).start()
    acc = acc + product(2, 0) + product(3, 0)
    relay(3, 3).wait_recv()
    acc = acc + product(3, 1)
    relay(2, 2).wait_recv()
    acc = acc + product(2, 1)

    def drain_gather(owns, zone):
        @pl.when(owns)
        def _():
            drain(full.at[0, pl.ds(AT[zone], WIDE[zone] - 1)], ag_recv.at[zone])

        @pl.when(jnp.logical_not(owns))
        def _():
            drain(full.at[0, pl.ds(AT[zone], WIDE[zone])], ag_recv.at[zone])

    drain_gather(owns_b, 1)
    relay(1, 1).start()
    acc = acc + product(1, 0)
    drain_gather(owns_a, 0)
    relay(0, 0).start()
    acc = acc + product(0, 0)
    relay(1, 1).wait_recv()
    acc = acc + product(1, 1)
    relay(0, 0).wait_recv()
    acc = acc + product(0, 1)
    out_ref[...] = (acc[0:4, 0:32] + acc[4:8, 32:64]) + (acc[8:12, 64:96] + acc[12:16, 96:128])

    for zone in range(4):
        core_copies[zone].wait_send()
        relay(zone, zone).wait_send()

    def drain_scatter(owns, zone):
        @pl.when(owns)
        def _():
            drain(mine.at[pl.ds(0, WIDE[zone] - 1)], rs_send.at[zone])

        @pl.when(jnp.logical_not(owns))
        def _():
            drain(mine.at[pl.ds(0, WIDE[zone])], rs_send.at[zone])

    drain_scatter(owns_a, 0)
    drain_scatter(owns_b, 1)
    drain(mine.at[pl.ds(0, 7)], rs_send.at[2])
    d_do(lambda copy: copy.wait_send())

    @pl.when(owns_ab)
    def _():
        drain(deep_ab, z_send.at[0])

    @pl.when(core == 0)
    def _():
        drain(deep_c, z_send.at[1])

    @pl.when(core == 1)
    def _():
        drain(deep_c.at[pl.ds(0, 3)], z_send.at[1])

    @pl.when(owns_a)
    def _():
        for _ in range(1):
            drain(full.at[0, pl.ds(0, 30)], ag_send.at[0])
            drain(full.at[0, pl.ds(0, 1)], ag_send.at[0])

    @pl.when(owns_b)
    def _():
        drain(full.at[0, pl.ds(0, 15)], ag_send.at[1])

    drain(full.at[0, pl.ds(0, 7)], ag_send.at[2])


def body(rhs, x_sep, x_loc, sep_sizes):
    vmem, hbm = pl.BlockSpec(memory_space=pltpu.VMEM), pl.BlockSpec(memory_space=pltpu.HBM)
    dma = pltpu.SemaphoreType.DMA
    blocks = functools.partial(pltpu.VMEM, dtype=F32)
    return pl.pallas_call(
        kernel,
        out_shape=jax.ShapeDtypeStruct((4, 32), F32),
        in_specs=[hbm] * 4,
        out_specs=vmem,
        scratch_shapes=[
            pltpu.VMEM((4, 32), BF16),
            pltpu.SMEM((9,), jnp.int32),
            pltpu.VMEM((2, 128, BLOCKS * 128), BF16),
            pltpu.VMEM((32, COLS % 128), BF16),
            pltpu.VMEM((128, LOC // 4), BF16),
            blocks((BLOCKS, 16, 128)),
            blocks((BLOCKS, 16, 128)),
            blocks((BLOCKS, 16, 128)),
            blocks((32, 16, 128)),
            blocks((8, 16, 128)),
            blocks((7, 2, 16, 128)),
            blocks((16, 128)),
            blocks((16, 128)),
            blocks((7, 16, 128)),
            blocks((7, 16, 128)),
            pltpu.VMEM((2, BLOCKS, 16, 128), BF16),
            dma((2,)),
            dma((2, 4, 5)),
            dma((4,)),
            dma((4,)),
            dma((4,)),
            dma((10,)),
            dma((10,)),
            dma((2,)),
            dma((2,)),
            dma((3,)),
            dma((3,)),
            dma((4,)),
            dma((4,)),
        ],
        compiler_params=pltpu.CompilerParams(
            collective_id=0, has_side_effects=True, vmem_limit_bytes=60 * 1024 * 1024
        ),
        name="xxt",
    )(rhs, sep_sizes, x_sep, x_loc)


def solution(mesh):
    placed = (P(None, "leaf"), P("leaf", None), P("leaf", None), P())
    return jax.shard_map(
        body, mesh=mesh, in_specs=placed, out_specs=P(None, "leaf"), check_vma=False
    )
```

```python
import functools

import jax
import jax.numpy as jnp
from jax import lax
from jax.experimental import pallas as pl
from jax.experimental.pallas import tpu as pltpu
from jax.sharding import PartitionSpec as P

MESH = pl.DeviceIdType.MESH
F32, BF16 = jnp.float32, jnp.bfloat16

CORE, X0, X1, Z0, Z1, Z2, Z3, Y0, Y1 = (1 << b for b in range(9))

ZONES = ((0, 100), (100, 50), (150, 64), (214, 16))
WIDE = (13, 7, 8, 2)
AT = (0, 13, 20, 28)
BLOCKS = 30
COLS = 29400
ENDS = (12800, 19200, 22400, 25600, 27200, 28000, 28800, 29200, 29400)
STARTS = (0,) + ENDS[:-1]
LOC = 4096


def window(zone, i):
    first, tiles = ZONES[zone]
    return first + (tiles * i) // 8


def column_of(zone, core, j):
    shape = (16, 128)
    i = 4 * core + lax.broadcasted_iota(jnp.int32, shape, 0) // 4
    lane = lax.broadcasted_iota(jnp.int32, shape, 1)
    first, tiles = ZONES[zone]
    start = first + (tiles * i) // 8
    end = first + (tiles * (i + 1)) // 8
    return (start + j) * 128 + lane, end * 128


def hops(mask):
    x, y = (mask // X0) % 4, (mask // Y0) % 4
    return (x > 0) + (x == 2) + (y > 0) + (y == 2) + (mask // Z0) % 2


def masks_of(bits):
    found = [0]
    for bit in bits:
        found += [m | bit for m in found]
    return sorted(found[1:], key=hops, reverse=True)


PLANE = masks_of((X0, X1, Z0, Y0, Y1))
PAIR = masks_of((X0, X1, Z0, Y0))
LINE = masks_of((X0, X1, Z0))
DEPTH = [m * Z1 for m in (4, 5, 3, 6, 2, 7, 1)]


def kernel(rhs_hbm, sizes_hbm, xsep_ref, xloc_ref, out_ref,
           rhs_ref, sizes_ref, xs, tail, xl, mine, send_core, recv_core, recv_ab, recv_c, recv_d, part_ab, part_c, deep_ab, deep_c, full,
           small_sem, load_sem, loc_sem, core_send, core_recv, rs_send, rs_recv, z_send, z_recv, ag_send, ag_recv,
           relay_send, relay_recv, token):
    me = lax.axis_index("leaf")

    def bit(b):
        return (me // b) % 2

    core = bit(CORE)
    y0, y1 = bit(Y0), bit(Y1)
    k = 2 * ((me // X0) % 4) + bit(Z0)
    delta = {b: (1 - 2 * bit(b)) * b for b in (CORE, X0, X1, Z0, Z1, Z2, Z3, Y0, Y1)}

    def partner(mask):
        other = me
        for b, d in delta.items():
            if mask & b:
                other = other + d
        return other

    def remote(src, dst, send, recv, device):
        return pltpu.make_async_remote_copy(
            src_ref=src, dst_ref=dst, send_sem=send, recv_sem=recv, device_id=(device,), device_id_type=MESH
        )

    def drain(ref, sem):
        pltpu.make_async_copy(ref, ref, sem).wait()

    depth = (me // Z1) % 8

    def along(step):
        return me + ((depth + step + 8) % 8 - depth) * Z1

    barrier = pltpu.get_barrier_semaphore()
    greeted = [partner(m) for m in PLANE] + [along(s) for s in (2, -2, 1, -1)] + [partner(CORE)]
    for device in greeted:
        pl.semaphore_signal(barrier, inc=1, device_id=(device,), device_id_type=MESH)

    rhs_copy = pltpu.make_async_copy(rhs_hbm, rhs_ref, small_sem.at[0])
    sizes_copy = pltpu.make_async_copy(sizes_hbm, sizes_ref, small_sem.at[1])
    rhs_copy.start()
    sizes_copy.start()

    loads = {}
    for zone in range(4):
        for half in (1, 0):
            owner = core if half == 0 else 1 - core
            group = []
            for s in range(4):
                begin0, begin1 = window(zone, s), window(zone, 4 + s)
                width = WIDE[zone] * 128
                at = AT[zone] * 128
                rows = pl.ds(32 * s, 32)
                sem = load_sem.at[half, zone, s]
                if zone == 3 and s == 3:
                    group.append((begin0, begin1, sem, rows, at, owner))
                    continue
                start = pl.multiple_of((begin0 + owner * (begin1 - begin0)) * 128, 128)
                copy = pltpu.make_async_copy(
                    xsep_ref.at[:, pl.ds(start, width)], xs.at[half, rows, pl.ds(at, width)], sem
                )
                copy.start()
                group.append(copy)
            loads[zone, half] = group

    def last_copies(half, last):
        begin0, begin1, sem, rows, at, owner = loads[3, half][3]
        if not last:
            return [pltpu.make_async_copy(
                xsep_ref.at[:, pl.ds(begin0 * 128, 256)], xs.at[half, rows, pl.ds(at, 256)], sem)]
        rest = COLS - (begin1 + 1) * 128
        return [
            pltpu.make_async_copy(
                xsep_ref.at[:, pl.ds(begin1 * 128, 128)], xs.at[half, rows, pl.ds(at, 128)], sem),
            pltpu.make_async_copy(
                xsep_ref.at[:, pl.ds((begin1 + 1) * 128, rest)], tail, load_sem.at[half, 3, 4]),
        ]

    def last_do(action):
        for half in (0, 1):
            owner = core if half == 0 else 1 - core
            for last in (False, True):
                @pl.when(owner == int(last))
                def _():
                    for copy in last_copies(half, last):
                        action(copy)

    last_do(lambda copy: copy.start())
    loc_copies = [
        pltpu.make_async_copy(xloc_ref.at[:, pl.ds(1024 * s, 1024)], xl.at[pl.ds(32 * s, 32), :], loc_sem.at[s])
        for s in range(4)
    ]
    for copy in loc_copies:
        copy.start()

    row = lax.broadcasted_iota(jnp.int32, (16, 128), 0)
    lane = lax.broadcasted_iota(jnp.int32, (16, 128), 1)
    diagonal = row // 4 == lane // 32
    pick_rows = (lax.broadcasted_iota(jnp.int32, (16, 4), 0) % 4 == lax.broadcasted_iota(jnp.int32, (16, 4), 1))
    pick_lanes = (lax.broadcasted_iota(jnp.int32, (32, 128), 1) % 32 == lax.broadcasted_iota(jnp.int32, (32, 128), 0))
    rhs_copy.wait()
    sizes_copy.wait()
    tall = jnp.dot(pick_rows.astype(BF16), rhs_ref[...], preferred_element_type=F32).astype(BF16)
    wide = jnp.dot(tall, pick_lanes.astype(BF16), preferred_element_type=F32)
    rhs16 = jnp.where(diagonal, wide, 0.0).astype(BF16)

    def contributions(zone, half, store):
        columns = pl.ds(AT[zone] * 128, WIDE[zone] * 128)
        product = jnp.dot(rhs16, xs[half, :, columns], preferred_element_type=F32)
        for j in range(WIDE[zone]):
            store[AT[zone] + j] = product[:, 128 * j : 128 * j + 128]

    def place_tail(half):
        @pl.when((core if half == 0 else 1 - core) == 1)
        def _():
            rest = jnp.concatenate([tail[...], jnp.zeros((32, 128 - tail.shape[1]), BF16)], axis=1)
            xs[half, 96:128, BLOCKS * 128 - 128 : BLOCKS * 128] = rest

    for zone in range(4):
        for half in (1, 0):
            for copy in loads[zone, half]:
                if not isinstance(copy, tuple):
                    copy.wait()
        if zone == 3:
            last_do(lambda copy: copy.wait())
            place_tail(1)
            place_tail(0)
        contributions(zone, 1, send_core)
        contributions(zone, 0, mine)

    pl.semaphore_wait(barrier, len(greeted))
    for step in (2, -2):
        pl.semaphore_signal(token, inc=1, device_id=(along(step),), device_id_type=MESH)

    sibling = partner(CORE)
    core_copies = []
    for zone in range(4):
        blocks = pl.ds(AT[zone], WIDE[zone])
        copy = remote(send_core.at[blocks], recv_core.at[blocks], core_send.at[zone], core_recv.at[zone], sibling)
        copy.start()
        core_copies.append(copy)

    base = me - me % Z1 + core - y1 * Y1 - y0 * Y0

    def place(kk):
        return (kk // 2) * X0 + (kk % 2) * Z0

    def owner_a(a):
        return base + (a % 2) * Y1 + core * Y0 + place(a // 2)

    def owner_b(b):
        return base + y1 * Y1 + (1 - core) * Y0 + place(b)

    def owner_c(d):
        return base + y1 * Y1 + y0 * Y0 + place(d)

    role_a = y0 == core
    a_mine = 2 * k + y1
    owns_a = jnp.logical_and(role_a, a_mine < WIDE[0])
    owns_b = jnp.logical_and(jnp.logical_not(role_a), k < WIDE[1])
    slot_a = 16 * y1 + 8 * y0 + k
    slot_b = 8 * y0 + k

    def scatter(zone, count, owner, slot, landing, sem):
        for j in range(count):
            block = AT[zone] + j
            to = owner(j)

            @pl.when(to == me)
            def _():
                landing[slot] = mine[block]

            @pl.when(to != me)
            def _():
                remote(mine.at[block], landing.at[slot], rs_send.at[sem], rs_recv.at[sem], to).start()

    for zone in range(4):
        core_copies[zone].wait_recv()
        for j in range(WIDE[zone]):
            block = AT[zone] + j
            mine[block] = mine[block] + recv_core[block]
        if zone == 0:
            scatter(0, WIDE[0], owner_a, slot_a, recv_ab, 0)
        elif zone == 1:
            scatter(1, WIDE[1], owner_b, slot_b, recv_ab, 1)
        elif zone == 2:
            scatter(2, WIDE[2], owner_c, k, recv_c, 2)

    def d_copy(n, mask):
        return remote(mine.at[pl.ds(AT[3], 2)], recv_d.at[n], rs_send.at[3 + n], rs_recv.at[3 + n], partner(mask))

    def d_do(action):
        for n, mask in enumerate(LINE):
            if mask & Z0:
                @pl.when(core == 0)
                def _():
                    action(d_copy(n, mask))
            else:
                action(d_copy(n, mask))

    d_do(lambda copy: copy.start())

    def total(landing, count):
        acc = [landing[i] for i in range(4)]
        for i in range(4, count):
            acc[i % 4] = acc[i % 4] + landing[i]
        return (acc[0] + acc[1]) + (acc[2] + acc[3])

    def deep_copies(src, landing, at):
        return [
            remote(src, landing.at[m // Z1 - 1], z_send.at[at], z_recv.at[at], partner(m)) for m in DEPTH
        ]

    pl.semaphore_wait(token, 2)

    drain(recv_c.at[pl.ds(0, 7)], rs_recv.at[2])
    part_c[...] = total(recv_c, 8)
    deep_c_copies = deep_copies(part_c, deep_c, 1)
    for m, copy in zip(DEPTH, deep_c_copies):
        if m & Z3:
            @pl.when(core == 0)
            def _():
                copy.start()
        else:
            copy.start()

    @pl.when(owns_a)
    def _():
        drain(recv_ab.at[pl.ds(0, 31)], rs_recv.at[0])
        part_ab[...] = total(recv_ab, 32)

    @pl.when(owns_b)
    def _():
        drain(recv_ab.at[pl.ds(0, 15)], rs_recv.at[1])
        part_ab[...] = total(recv_ab, 16)

    owns_ab = jnp.logical_or(owns_a, owns_b)

    @pl.when(owns_ab)
    def _():
        for copy in deep_copies(part_ab, deep_ab, 0):
            copy.start()

    def active(columns, zone):
        lo, hi = ZONES[zone][0] * 128, sum(ZONES[zone]) * 128
        keep = None
        for level in range(9):
            if STARTS[level] < hi and ENDS[level] > lo:
                limit = STARTS[level] + sizes_ref[level]
                inside = jnp.logical_and(
                    jnp.logical_and(columns >= STARTS[level], columns < ENDS[level]), columns < limit)
                keep = inside if keep is None else jnp.logical_or(keep, inside)
        return keep

    def rounded(values, columns, end, zone):
        keep = jnp.logical_and(active(columns, zone), columns < end)
        return jnp.where(keep, values, 0.0).astype(BF16)

    d_do(lambda copy: copy.wait_recv())
    for j in range(2):
        columns, end = column_of(3, core, j)
        value = mine[AT[3] + j]
        for n, mask in enumerate(LINE):
            if mask & Z0:
                bound = jnp.where(core == 0, ENDS[5], 0)
            else:
                bound = ENDS[6] if mask & X1 else ENDS[7]
            value = value + jnp.where(columns < bound, recv_d[n, j], 0.0)
        full[0, AT[3] + j] = rounded(value, columns, end, 3)

    def relay(zone, at):
        blocks = pl.ds(AT[zone], WIDE[zone])
        return remote(full.at[0, blocks], full.at[1, blocks], relay_send.at[at], relay_recv.at[at], sibling)

    relay(3, 3).start()

    for copy in loc_copies:
        copy.wait()
    interior = jnp.dot(rhs16, xl[...], preferred_element_type=F32).astype(BF16)
    contract = (((1,), (1,)), ((), ()))
    acc = lax.dot_general(interior, xl[...], contract, preferred_element_type=F32)

    def product(zone, half):
        blocks = jnp.concatenate([full[half, AT[zone] + j] for j in range(WIDE[zone])], axis=1)
        columns = pl.ds(AT[zone] * 128, WIDE[zone] * 128)
        return lax.dot_general(blocks, xs[half, :, columns], contract, preferred_element_type=F32)

    def deep_total(part, landing):
        value = part[...]
        for i in range(7):
            value = value + landing[i]
        return value

    def gather(block, masks, sem):
        for mask in masks:
            remote(full.at[0, block], full.at[0, block], ag_send.at[sem], ag_recv.at[sem], partner(mask)).start()

    @pl.when(core == 0)
    def _():
        drain(deep_c, z_recv.at[1])

    @pl.when(core == 1)
    def _():
        drain(deep_c.at[pl.ds(0, 3)], z_recv.at[1])

    columns, end = column_of(2, core, k)
    value = part_c[...]
    for m in range(1, 8):
        bound = ENDS[4] if m == 1 else ENDS[3] if m < 4 else jnp.where(core == 0, ENDS[2], 0)
        value = value + jnp.where(columns < bound, deep_c[m - 1], 0.0)
    full[0, AT[2] + k] = rounded(value, columns, end, 2)
    gather(AT[2] + k, LINE, 2)

    @pl.when(owns_ab)
    def _():
        drain(deep_ab, z_recv.at[0])

    @pl.when(owns_a)
    def _():
        columns, end = column_of(0, core, a_mine)
        full[0, a_mine] = rounded(deep_total(part_ab, deep_ab), columns, end, 0)
        gather(a_mine, PLANE, 0)

    @pl.when(owns_b)
    def _():
        columns, end = column_of(1, core, k)
        full[0, AT[1] + k] = rounded(deep_total(part_ab, deep_ab), columns, end, 1)
        gather(AT[1] + k, PAIR, 1)

    drain(full.at[0, pl.ds(AT[2], 7)], ag_recv.at[2])
    relay(2, 2).start()
    acc = acc + product(2, 0) + product(3, 0)
    relay(3, 3).wait_recv()
    acc = acc + product(3, 1)
    relay(2, 2).wait_recv()
    acc = acc + product(2, 1)

    def drain_gather(owns, zone):
        @pl.when(owns)
        def _():
            drain(full.at[0, pl.ds(AT[zone], WIDE[zone] - 1)], ag_recv.at[zone])

        @pl.when(jnp.logical_not(owns))
        def _():
            drain(full.at[0, pl.ds(AT[zone], WIDE[zone])], ag_recv.at[zone])

    drain_gather(owns_b, 1)
    relay(1, 1).start()
    acc = acc + product(1, 0)
    drain_gather(owns_a, 0)
    relay(0, 0).start()
    acc = acc + product(0, 0)
    relay(1, 1).wait_recv()
    acc = acc + product(1, 1)
    relay(0, 0).wait_recv()
    acc = acc + product(0, 1)
    out_ref[...] = (acc[0:4, 0:32] + acc[4:8, 32:64]) + (acc[8:12, 64:96] + acc[12:16, 96:128])

    for zone in range(4):
        core_copies[zone].wait_send()
        relay(zone, zone).wait_send()

    def drain_scatter(owns, zone):
        @pl.when(owns)
        def _():
            drain(mine.at[pl.ds(0, WIDE[zone] - 1)], rs_send.at[zone])

        @pl.when(jnp.logical_not(owns))
        def _():
            drain(mine.at[pl.ds(0, WIDE[zone])], rs_send.at[zone])

    drain_scatter(owns_a, 0)
    drain_scatter(owns_b, 1)
    drain(mine.at[pl.ds(0, 7)], rs_send.at[2])
    d_do(lambda copy: copy.wait_send())

    @pl.when(owns_ab)
    def _():
        drain(deep_ab, z_send.at[0])

    @pl.when(core == 0)
    def _():
        drain(deep_c, z_send.at[1])

    @pl.when(core == 1)
    def _():
        drain(deep_c.at[pl.ds(0, 3)], z_send.at[1])

    @pl.when(owns_a)
    def _():
        for _ in range(1):
            drain(full.at[0, pl.ds(0, 30)], ag_send.at[0])
            drain(full.at[0, pl.ds(0, 1)], ag_send.at[0])

    @pl.when(owns_b)
    def _():
        drain(full.at[0, pl.ds(0, 15)], ag_send.at[1])

    drain(full.at[0, pl.ds(0, 7)], ag_send.at[2])


def body(rhs, x_sep, x_loc, sep_sizes):
    vmem, hbm = pl.BlockSpec(memory_space=pltpu.VMEM), pl.BlockSpec(memory_space=pltpu.HBM)
    dma = pltpu.SemaphoreType.DMA
    blocks = functools.partial(pltpu.VMEM, dtype=F32)
    return pl.pallas_call(
        kernel,
        out_shape=pltpu.VMEM((4, 32), F32),
        in_specs=[hbm] * 4,
        out_specs=vmem,
        scratch_shapes=[
            pltpu.VMEM((4, 32), BF16),
            pltpu.SMEM((9,), jnp.int32),
            pltpu.VMEM((2, 128, BLOCKS * 128), BF16),
            pltpu.VMEM((32, COLS % 128), BF16),
            pltpu.VMEM((128, LOC // 4), BF16),
            blocks((BLOCKS, 16, 128)),
            blocks((BLOCKS, 16, 128)),
            blocks((BLOCKS, 16, 128)),
            blocks((32, 16, 128)),
            blocks((8, 16, 128)),
            blocks((7, 2, 16, 128)),
            blocks((16, 128)),
            blocks((16, 128)),
            blocks((7, 16, 128)),
            blocks((7, 16, 128)),
            pltpu.VMEM((2, BLOCKS, 16, 128), BF16),
            dma((2,)),
            dma((2, 4, 5)),
            dma((4,)),
            dma((4,)),
            dma((4,)),
            dma((10,)),
            dma((10,)),
            dma((2,)),
            dma((2,)),
            dma((3,)),
            dma((3,)),
            dma((4,)),
            dma((4,)),
            pltpu.SemaphoreType.REGULAR,
        ],
        compiler_params=pltpu.CompilerParams(
            collective_id=0, has_side_effects=True, vmem_limit_bytes=60 * 1024 * 1024
        ),
        name="xxt",
    )(rhs, sep_sizes, x_sep, x_loc)


def solution(mesh):
    placed = (P(None, "leaf"), P("leaf", None), P("leaf", None), P())
    return jax.shard_map(
        body, mesh=mesh, in_specs=placed, out_specs=P(None, "leaf"), check_vma=False
    )
```

```python
import functools

import jax
import jax.numpy as jnp
from jax import lax
from jax.experimental import pallas as pl
from jax.experimental.pallas import tpu as pltpu
from jax.sharding import PartitionSpec as P

MESH = pl.DeviceIdType.MESH
F32, BF16 = jnp.float32, jnp.bfloat16

CORE, X0, X1, Z0, Z1, Z2, Z3, Y0, Y1 = (1 << b for b in range(9))

ZONES = ((0, 100), (100, 50), (150, 64), (212, 18))
WIDE = (13, 7, 8, 3)
AT = (0, 13, 20, 28)
BLOCKS = 31
KEEP = ((0, 12800), (12800, 19200), (19200, 27200), (27200, 29400))
COLS = 29400
ENDS = (12800, 19200, 22400, 25600, 27200, 28000, 28800, 29200, 29400)
STARTS = (0,) + ENDS[:-1]
LOC = 4096


def window(zone, i):
    first, tiles = ZONES[zone]
    return first + (tiles * i) // 8


def column_of(zone, core, j):
    shape = (16, 128)
    i = 4 * core + lax.broadcasted_iota(jnp.int32, shape, 0) // 4
    lane = lax.broadcasted_iota(jnp.int32, shape, 1)
    first, tiles = ZONES[zone]
    start = first + (tiles * i) // 8
    end = first + (tiles * (i + 1)) // 8
    return (start + j) * 128 + lane, end * 128


def hops(mask):
    x, y, z = (mask // X0) % 4, (mask // Y0) % 4, (mask // Z0) % 4
    return (x > 0) + (x == 2) + (y > 0) + (y == 2) + z


def masks_of(bits):
    found = [0]
    for bit in bits:
        found += [m | bit for m in found]
    return sorted(found[1:], key=hops, reverse=True)


PLANE = masks_of((X0, X1, Z0, Y0, Y1))
PAIR = masks_of((X0, X1, Z0, Y0))
LINE = masks_of((X0, X1, Z0))
SLAB = masks_of((X0, X1, Z0, Z1))
DEPTH = [m * Z1 for m in (4, 5, 3, 6, 2, 7, 1)]
DEPTH_C = [m * Z1 for m in (4, 2, 6)]


def kernel(rhs_hbm, sizes_hbm, xsep_ref, xloc_ref, out_ref,
           rhs_ref, sizes_ref, xs, tail, xl, mine, send_core, recv_core, recv_ab, recv_c, recv_d, part_ab, part_c, deep_ab, deep_c, full,
           small_sem, load_sem, loc_sem, core_send, core_recv, rs_send, rs_recv, z_send, z_recv, ag_send, ag_recv,
           relay_send, relay_recv, token):
    me = lax.axis_index("leaf")

    def bit(b):
        return (me // b) % 2

    core = bit(CORE)
    y0, y1, z1 = bit(Y0), bit(Y1), bit(Z1)
    k = 2 * ((me // X0) % 4) + bit(Z0)
    delta = {b: (1 - 2 * bit(b)) * b for b in (CORE, X0, X1, Z0, Z1, Z2, Z3, Y0, Y1)}

    def partner(mask):
        other = me
        for b, d in delta.items():
            if mask & b:
                other = other + d
        return other

    def remote(src, dst, send, recv, device):
        return pltpu.make_async_remote_copy(
            src_ref=src, dst_ref=dst, send_sem=send, recv_sem=recv, device_id=(device,), device_id_type=MESH
        )

    def drain(ref, sem):
        pltpu.make_async_copy(ref, ref, sem).wait()

    depth = (me // Z1) % 8

    def along(step):
        return me + ((depth + step + 8) % 8 - depth) * Z1

    barrier = pltpu.get_barrier_semaphore()
    greeted = [partner(m) for m in PLANE + [m | Z1 for m in LINE]]
    greeted += [along(s) for s in (2, -2, 1, -1)] + [partner(CORE)]
    for device in greeted:
        pl.semaphore_signal(barrier, inc=1, device_id=(device,), device_id_type=MESH)

    rhs_copy = pltpu.make_async_copy(rhs_hbm, rhs_ref, small_sem.at[0])
    sizes_copy = pltpu.make_async_copy(sizes_hbm, sizes_ref, small_sem.at[1])
    rhs_copy.start()
    sizes_copy.start()

    loads = {}
    for zone in range(4):
        for half in (1, 0):
            owner = core if half == 0 else 1 - core
            group = []
            for s in range(4):
                begin0, begin1 = window(zone, s), window(zone, 4 + s)
                width = WIDE[zone] * 128
                at = AT[zone] * 128
                rows = pl.ds(32 * s, 32)
                sem = load_sem.at[half, zone, s]
                if zone == 3 and s == 3:
                    group.append((begin0, begin1, sem, rows, at, owner))
                    continue
                start = pl.multiple_of((begin0 + owner * (begin1 - begin0)) * 128, 128)
                copy = pltpu.make_async_copy(
                    xsep_ref.at[:, pl.ds(start, width)], xs.at[half, rows, pl.ds(at, width)], sem
                )
                copy.start()
                group.append(copy)
            loads[zone, half] = group

    def last_copies(half, last):
        begin0, begin1, sem, rows, at, owner = loads[3, half][3]
        if not last:
            return [pltpu.make_async_copy(
                xsep_ref.at[:, pl.ds(begin0 * 128, 384)], xs.at[half, rows, pl.ds(at, 384)], sem)]
        rest = COLS - (begin1 + 2) * 128
        return [
            pltpu.make_async_copy(
                xsep_ref.at[:, pl.ds(begin1 * 128, 256)], xs.at[half, rows, pl.ds(at, 256)], sem),
            pltpu.make_async_copy(
                xsep_ref.at[:, pl.ds((begin1 + 2) * 128, rest)], tail, load_sem.at[half, 3, 4]),
        ]

    def last_do(action):
        for half in (0, 1):
            owner = core if half == 0 else 1 - core
            for last in (False, True):
                @pl.when(owner == int(last))
                def _():
                    for copy in last_copies(half, last):
                        action(copy)

    last_do(lambda copy: copy.start())
    loc_copies = [
        pltpu.make_async_copy(xloc_ref.at[:, pl.ds(1024 * s, 1024)], xl.at[pl.ds(32 * s, 32), :], loc_sem.at[s])
        for s in range(4)
    ]
    for copy in loc_copies:
        copy.start()

    row = lax.broadcasted_iota(jnp.int32, (16, 128), 0)
    lane = lax.broadcasted_iota(jnp.int32, (16, 128), 1)
    diagonal = row // 4 == lane // 32
    pick_rows = (lax.broadcasted_iota(jnp.int32, (16, 4), 0) % 4 == lax.broadcasted_iota(jnp.int32, (16, 4), 1))
    pick_lanes = (lax.broadcasted_iota(jnp.int32, (32, 128), 1) % 32 == lax.broadcasted_iota(jnp.int32, (32, 128), 0))
    rhs_copy.wait()
    sizes_copy.wait()
    tall = jnp.dot(pick_rows.astype(BF16), rhs_ref[...], preferred_element_type=F32).astype(BF16)
    wide = jnp.dot(tall, pick_lanes.astype(BF16), preferred_element_type=F32)
    rhs16 = jnp.where(diagonal, wide, 0.0).astype(BF16)

    def contributions(zone, half, store):
        columns = pl.ds(AT[zone] * 128, WIDE[zone] * 128)
        product = jnp.dot(rhs16, xs[half, :, columns], preferred_element_type=F32)
        for j in range(WIDE[zone]):
            store[AT[zone] + j] = product[:, 128 * j : 128 * j + 128]

    def place_tail(half):
        @pl.when((core if half == 0 else 1 - core) == 1)
        def _():
            rest = jnp.concatenate([tail[...], jnp.zeros((32, 128 - tail.shape[1]), BF16)], axis=1)
            xs[half, 96:128, BLOCKS * 128 - 128 : BLOCKS * 128] = rest

    for zone in range(4):
        for half in (1, 0):
            for copy in loads[zone, half]:
                if not isinstance(copy, tuple):
                    copy.wait()
        if zone == 3:
            last_do(lambda copy: copy.wait())
            place_tail(1)
            place_tail(0)
        contributions(zone, 1, send_core)
        contributions(zone, 0, mine)

    pl.semaphore_wait(barrier, len(greeted))
    for step in (2, -2):
        pl.semaphore_signal(token, inc=1, device_id=(along(step),), device_id_type=MESH)

    sibling = partner(CORE)
    core_copies = []
    for zone in range(4):
        blocks = pl.ds(AT[zone], WIDE[zone])
        copy = remote(send_core.at[blocks], recv_core.at[blocks], core_send.at[zone], core_recv.at[zone], sibling)
        copy.start()
        core_copies.append(copy)

    base = me - me % Z1 + core - y1 * Y1 - y0 * Y0

    def place(kk):
        return (kk // 2) * X0 + (kk % 2) * Z0

    def owner_a(a):
        return base + (a % 2) * Y1 + core * Y0 + place(a // 2)

    def owner_b(b):
        return base + y1 * Y1 + (1 - core) * Y0 + place(b)

    def owner_c(d):
        return base + y1 * Y1 + y0 * Y0 + (core - z1) * Z1 + place(d)

    role_a = y0 == core
    a_mine = 2 * k + y1
    owns_a = jnp.logical_and(role_a, a_mine < WIDE[0])
    owns_b = jnp.logical_and(jnp.logical_not(role_a), k < WIDE[1])
    slot_a = 16 * y1 + 8 * y0 + k
    slot_b = 8 * y0 + k
    slot_c = 8 * z1 + k
    owns_c = z1 == core

    def scatter(zone, count, owner, slot, landing, sem):
        for j in range(count):
            block = AT[zone] + j
            to = owner(j)

            @pl.when(to == me)
            def _():
                landing[slot] = mine[block]

            @pl.when(to != me)
            def _():
                remote(mine.at[block], landing.at[slot], rs_send.at[sem], rs_recv.at[sem], to).start()

    for zone in range(4):
        core_copies[zone].wait_recv()
        for j in range(WIDE[zone]):
            block = AT[zone] + j
            mine[block] = mine[block] + recv_core[block]
        if zone == 0:
            scatter(0, WIDE[0], owner_a, slot_a, recv_ab, 0)
        elif zone == 1:
            scatter(1, WIDE[1], owner_b, slot_b, recv_ab, 1)
        elif zone == 2:
            scatter(2, WIDE[2], owner_c, slot_c, recv_c, 2)

    def d_copy(n, mask):
        return remote(mine.at[pl.ds(AT[3], WIDE[3])], recv_d.at[n], rs_send.at[3 + n], rs_recv.at[3 + n], partner(mask))

    def d_do(action):
        for n, mask in enumerate(LINE):
            if mask & Z0:
                @pl.when(core == 0)
                def _():
                    action(d_copy(n, mask))
            else:
                action(d_copy(n, mask))

    def total(landing, count):
        acc = [landing[i] for i in range(4)]
        for i in range(4, count):
            acc[i % 4] = acc[i % 4] + landing[i]
        return (acc[0] + acc[1]) + (acc[2] + acc[3])

    def deep_copies(src, landing, at):
        return [
            remote(src, landing.at[m // Z1 - 1], z_send.at[at], z_recv.at[at], partner(m)) for m in DEPTH
        ]

    pl.semaphore_wait(token, 2)

    @pl.when(owns_a)
    def _():
        drain(recv_ab.at[pl.ds(0, 31)], rs_recv.at[0])
        part_ab[...] = total(recv_ab, 32)

    @pl.when(owns_b)
    def _():
        drain(recv_ab.at[pl.ds(0, 15)], rs_recv.at[1])
        part_ab[...] = total(recv_ab, 16)

    owns_ab = jnp.logical_or(owns_a, owns_b)

    @pl.when(owns_ab)
    def _():
        for copy in deep_copies(part_ab, deep_ab, 0):
            copy.start()

    def c_far(action):
        for m in DEPTH_C:
            if m & Z3:
                @pl.when(core == 0)
                def _():
                    action(m)
            else:
                action(m)

    @pl.when(owns_c)
    def _():
        drain(recv_c.at[pl.ds(0, 15)], rs_recv.at[2])
        part_c[...] = total(recv_c, 16)
        c_far(lambda m: remote(
            part_c, deep_c.at[m // Z2 - 1], z_send.at[1], z_recv.at[1], partner(m)).start())

    d_do(lambda copy: copy.start())

    def active(columns, zone):
        lo, hi = ZONES[zone][0] * 128, sum(ZONES[zone]) * 128
        keep = None
        for level in range(9):
            if STARTS[level] < hi and ENDS[level] > lo:
                limit = STARTS[level] + sizes_ref[level]
                inside = jnp.logical_and(
                    jnp.logical_and(columns >= STARTS[level], columns < ENDS[level]), columns < limit)
                keep = inside if keep is None else jnp.logical_or(keep, inside)
        lo, hi = KEEP[zone]
        return jnp.logical_and(keep, jnp.logical_and(columns >= lo, columns < hi))

    def rounded(values, columns, end, zone):
        keep = jnp.logical_and(active(columns, zone), columns < end)
        return jnp.where(keep, values, 0.0).astype(BF16)

    d_do(lambda copy: copy.wait_recv())
    for j in range(WIDE[3]):
        columns, end = column_of(3, core, j)
        value = mine[AT[3] + j]
        for n, mask in enumerate(LINE):
            if mask & Z0:
                bound = jnp.where(core == 0, ENDS[5], 0)
            else:
                bound = ENDS[6] if mask & X1 else ENDS[7]
            value = value + jnp.where(columns < bound, recv_d[n, j], 0.0)
        full[0, AT[3] + j] = rounded(value, columns, end, 3)

    def relay(zone, at):
        blocks = pl.ds(AT[zone], WIDE[zone])
        return remote(full.at[0, blocks], full.at[1, blocks], relay_send.at[at], relay_recv.at[at], sibling)

    relay(3, 3).start()

    for copy in loc_copies:
        copy.wait()
    interior = jnp.dot(rhs16, xl[...], preferred_element_type=F32).astype(BF16)
    contract = (((1,), (1,)), ((), ()))
    acc = lax.dot_general(interior, xl[...], contract, preferred_element_type=F32)

    def product(zone, half):
        blocks = jnp.concatenate([full[half, AT[zone] + j] for j in range(WIDE[zone])], axis=1)
        columns = pl.ds(AT[zone] * 128, WIDE[zone] * 128)
        return lax.dot_general(blocks, xs[half, :, columns], contract, preferred_element_type=F32)

    def deep_total(part, landing):
        value = part[...]
        for i in range(7):
            value = value + landing[i]
        return value

    def gather(block, masks, sem):
        for mask in masks:
            remote(full.at[0, block], full.at[0, block], ag_send.at[sem], ag_recv.at[0, sem], partner(mask)).start()
            remote(full.at[0, block], full.at[1, block], ag_send.at[sem], ag_recv.at[1, sem], partner(mask | CORE)).start()
        remote(full.at[0, block], full.at[1, block], ag_send.at[sem], ag_recv.at[1, sem], partner(CORE)).start()

    @pl.when(owns_ab)
    def _():
        drain(deep_ab, z_recv.at[0])

    @pl.when(owns_a)
    def _():
        columns, end = column_of(0, core, a_mine)
        full[0, a_mine] = rounded(deep_total(part_ab, deep_ab), columns, end, 0)
        gather(a_mine, PLANE, 0)

    @pl.when(owns_b)
    def _():
        columns, end = column_of(1, core, k)
        full[0, AT[1] + k] = rounded(deep_total(part_ab, deep_ab), columns, end, 1)
        gather(AT[1] + k, PAIR, 1)

    @pl.when(owns_c)
    def _():
        @pl.when(core == 0)
        def _():
            drain(deep_c, z_recv.at[1])

        @pl.when(core == 1)
        def _():
            drain(deep_c.at[pl.ds(0, 1)], z_recv.at[1])

        columns, end = column_of(2, core, k)
        value = part_c[...]
        for m in range(1, 4):
            bound = ENDS[3] if m == 1 else jnp.where(core == 0, ENDS[2], 0)
            value = value + jnp.where(columns < bound, deep_c[m - 1], 0.0)
        full[0, AT[2] + k] = rounded(value, columns, end, 2)
        gather(AT[2] + k, SLAB, 2)

    acc = acc + product(3, 0)
    relay(3, 3).wait_recv()
    acc = acc + product(3, 1)

    for zone in range(4):
        core_copies[zone].wait_send()
    relay(3, 3).wait_send()

    def drain_scatter(owns, zone):
        @pl.when(owns)
        def _():
            drain(mine.at[pl.ds(0, WIDE[zone] - 1)], rs_send.at[zone])

        @pl.when(jnp.logical_not(owns))
        def _():
            drain(mine.at[pl.ds(0, WIDE[zone])], rs_send.at[zone])

    drain_scatter(owns_a, 0)
    drain_scatter(owns_b, 1)
    drain_scatter(owns_c, 2)
    d_do(lambda copy: copy.wait_send())

    @pl.when(owns_ab)
    def _():
        drain(deep_ab, z_send.at[0])

    @pl.when(jnp.logical_and(owns_c, core == 0))
    def _():
        drain(deep_c, z_send.at[1])

    @pl.when(jnp.logical_and(owns_c, core == 1))
    def _():
        drain(deep_c.at[pl.ds(0, 1)], z_send.at[1])

    def drain_gather(owns, zone):
        @pl.when(owns)
        def _():
            drain(full.at[0, pl.ds(AT[zone], WIDE[zone] - 1)], ag_recv.at[0, zone])

        @pl.when(jnp.logical_not(owns))
        def _():
            drain(full.at[0, pl.ds(AT[zone], WIDE[zone])], ag_recv.at[0, zone])

    drain_gather(owns_b, 1)
    acc = acc + product(1, 0)
    drain(full.at[1, pl.ds(AT[1], WIDE[1])], ag_recv.at[1, 1])
    acc = acc + product(1, 1)
    drain_gather(owns_c, 2)
    acc = acc + product(2, 0)
    drain(full.at[1, pl.ds(AT[2], WIDE[2])], ag_recv.at[1, 2])
    acc = acc + product(2, 1)
    drain_gather(owns_a, 0)
    acc = acc + product(0, 0)
    drain(full.at[1, pl.ds(AT[0], WIDE[0])], ag_recv.at[1, 0])
    acc = acc + product(0, 1)
    out_ref[...] = (acc[0:4, 0:32] + acc[4:8, 32:64]) + (acc[8:12, 64:96] + acc[12:16, 96:128])

    @pl.when(owns_a)
    def _():
        drain(full, ag_send.at[0])
        drain(full.at[0, pl.ds(0, 1)], ag_send.at[0])

    @pl.when(owns_b)
    def _():
        drain(full.at[0, pl.ds(0, 31)], ag_send.at[1])

    @pl.when(owns_c)
    def _():
        drain(full.at[0, pl.ds(0, 31)], ag_send.at[2])


def body(rhs, x_sep, x_loc, sep_sizes):
    vmem, hbm = pl.BlockSpec(memory_space=pltpu.VMEM), pl.BlockSpec(memory_space=pltpu.HBM)
    dma = pltpu.SemaphoreType.DMA
    blocks = functools.partial(pltpu.VMEM, dtype=F32)
    return pl.pallas_call(
        kernel,
        out_shape=pltpu.VMEM((4, 32), F32),
        in_specs=[hbm] * 4,
        out_specs=vmem,
        scratch_shapes=[
            pltpu.VMEM((4, 32), BF16),
            pltpu.SMEM((9,), jnp.int32),
            pltpu.VMEM((2, 128, BLOCKS * 128), BF16),
            pltpu.VMEM((32, COLS % 128), BF16),
            pltpu.VMEM((128, LOC // 4), BF16),
            blocks((BLOCKS, 16, 128)),
            blocks((BLOCKS, 16, 128)),
            blocks((BLOCKS, 16, 128)),
            blocks((32, 16, 128)),
            blocks((16, 16, 128)),
            blocks((7, WIDE[3], 16, 128)),
            blocks((16, 128)),
            blocks((16, 128)),
            blocks((7, 16, 128)),
            blocks((3, 16, 128)),
            pltpu.VMEM((2, BLOCKS, 16, 128), BF16),
            dma((2,)),
            dma((2, 4, 5)),
            dma((4,)),
            dma((4,)),
            dma((4,)),
            dma((10,)),
            dma((10,)),
            dma((2,)),
            dma((2,)),
            dma((3,)),
            dma((2, 3)),
            dma((4,)),
            dma((4,)),
            pltpu.SemaphoreType.REGULAR,
        ],
        compiler_params=pltpu.CompilerParams(
            collective_id=0, has_side_effects=True, vmem_limit_bytes=60 * 1024 * 1024
        ),
        name="xxt",
    )(rhs, sep_sizes, x_sep, x_loc)


def solution(mesh):
    placed = (P(None, "leaf"), P("leaf", None), P("leaf", None), P())
    return jax.shard_map(
        body, mesh=mesh, in_specs=placed, out_specs=P(None, "leaf"), check_vma=False
    )
```

```python
import functools

import jax
import jax.numpy as jnp
from jax import lax
from jax.experimental import pallas as pl
from jax.experimental.pallas import tpu as pltpu
from jax.sharding import PartitionSpec as P

MESH = pl.DeviceIdType.MESH
F32, BF16 = jnp.float32, jnp.bfloat16

CORE, X0, X1, Z0, Z1, Z2, Z3, Y0, Y1 = (1 << b for b in range(9))

ZONES = ((0, 100), (100, 50), (150, 64), (212, 18))
WIDE = (13, 7, 8, 3)
AT = (0, 13, 20, 28)
BLOCKS = 31
BEGIN = (0, 50, 75, 107)
TILES = 116
KEEP = ((0, 12800), (12800, 19200), (19200, 27200), (27200, 29400))
COLS = 29400
ENDS = (12800, 19200, 22400, 25600, 27200, 28000, 28800, 29200, 29400)
STARTS = (0,) + ENDS[:-1]
LOC = 4096


def window(zone, i):
    first, tiles = ZONES[zone]
    return first + (tiles * i) // 8


def column_of(zone, core, j):
    shape = (16, 128)
    i = 4 * core + lax.broadcasted_iota(jnp.int32, shape, 0) // 4
    lane = lax.broadcasted_iota(jnp.int32, shape, 1)
    first, tiles = ZONES[zone]
    start = first + (tiles * i) // 8
    end = first + (tiles * (i + 1)) // 8
    return (start + j) * 128 + lane, end * 128


def hops(mask):
    x, y, z = (mask // X0) % 4, (mask // Y0) % 4, (mask // Z0) % 4
    return (x > 0) + (x == 2) + (y > 0) + (y == 2) + z


def masks_of(bits):
    found = [0]
    for bit in bits:
        found += [m | bit for m in found]
    return sorted(found[1:], key=hops, reverse=True)


PLANE = masks_of((X0, X1, Z0, Y0, Y1))
PAIR = masks_of((X0, X1, Z0, Y0))
LINE = masks_of((X0, X1, Z0))
SLAB = masks_of((X0, X1, Z0, Z1))
DEPTH = [m * Z1 for m in (4, 5, 3, 6, 2, 7, 1)]
DEPTH_C = [m * Z1 for m in (4, 2, 6)]


def kernel(rhs_hbm, sizes_hbm, xsep_ref, xloc_ref, out_ref,
           rhs_ref, sizes_ref, xs, tail, xl, mine, send_core, recv_core, recv_ab, recv_c, recv_d, part_ab, part_c, deep_ab, deep_c, full,
           small_sem, load_sem, loc_sem, core_send, core_recv, rs_send, rs_recv, z_send, z_recv, ag_send, ag_recv,
           relay_send, relay_recv, token):
    me = lax.axis_index("leaf")

    def bit(b):
        return (me // b) % 2

    core = bit(CORE)
    y0, y1, z1 = bit(Y0), bit(Y1), bit(Z1)
    k = 2 * ((me // X0) % 4) + bit(Z0)
    delta = {b: (1 - 2 * bit(b)) * b for b in (CORE, X0, X1, Z0, Z1, Z2, Z3, Y0, Y1)}

    def partner(mask):
        other = me
        for b, d in delta.items():
            if mask & b:
                other = other + d
        return other

    def remote(src, dst, send, recv, device):
        return pltpu.make_async_remote_copy(
            src_ref=src, dst_ref=dst, send_sem=send, recv_sem=recv, device_id=(device,), device_id_type=MESH
        )

    def drain(ref, sem):
        pltpu.make_async_copy(ref, ref, sem).wait()

    base = me - me % Z1 + core - y1 * Y1 - y0 * Y0

    def place(kk):
        return (kk // 2) * X0 + (kk % 2) * Z0

    def owner_a(a):
        return base + (a % 2) * Y1 + core * Y0 + place(a // 2)

    def owner_b(b):
        return base + y1 * Y1 + (1 - core) * Y0 + place(b)

    def owner_c(d):
        return base + y1 * Y1 + y0 * Y0 + (core - z1) * Z1 + place(d)

    role_a = y0 == core
    a_mine = 2 * k + y1
    owns_a = jnp.logical_and(role_a, a_mine < WIDE[0])
    owns_b = jnp.logical_and(jnp.logical_not(role_a), k < WIDE[1])
    slot_a = 16 * y1 + 8 * y0 + k
    slot_b = 8 * y0 + k
    slot_c = 8 * z1 + k
    owns_c = z1 == core
    owns_ab = jnp.logical_or(owns_a, owns_b)

    depth = (me // Z1) % 8

    def along(step):
        return me + ((depth + step + 8) % 8 - depth) * Z1

    barrier = pltpu.get_barrier_semaphore()

    def greet(devices):
        for device in devices:
            pl.semaphore_signal(barrier, inc=1, device_id=(device,), device_id_type=MESH)

    def count(flag):
        return flag.astype(jnp.int32)

    @pl.when(owns_a)
    def _():
        greet(partner(m) for m in PLANE)

    @pl.when(owns_b)
    def _():
        greet(partner(m) for m in PAIR)

    @pl.when(owns_c)
    def _():
        greet(partner(m) for m in SLAB)

    @pl.when(jnp.logical_not(owns_ab))
    def _():
        greet(partner(m) for m in LINE)

    greet([along(s) for s in (2, -2, 1, -1)] + [partner(CORE)])
    line_owners = 7 - count(role_a) * y1
    greetings = (
        (WIDE[0] - count(owns_a)) + (WIDE[1] - count(owns_b)) + (WIDE[2] - count(owns_c))
        + (8 - line_owners - (1 - count(owns_ab))) + 5
    )

    rhs_copy = pltpu.make_async_copy(rhs_hbm, rhs_ref, small_sem.at[0])
    sizes_copy = pltpu.make_async_copy(sizes_hbm, sizes_ref, small_sem.at[1])
    rhs_copy.start()
    sizes_copy.start()

    def load(zone, half, width):
        first, tiles = ZONES[zone]
        owner = core if half == 0 else 1 - core
        start = pl.multiple_of((first + owner * (tiles // 2)) * 128, 128)
        return pltpu.make_async_copy(
            xsep_ref.at[:, pl.ds(start, width)], xs.at[half, :, pl.ds(BEGIN[zone] * 128, width)],
            load_sem.at[half, zone])

    def load_last(half, action):
        @pl.when((core if half == 0 else 1 - core) == 0)
        def _():
            action(load(3, half, 9 * 128))

        @pl.when((core if half == 0 else 1 - core) == 1)
        def _():
            action(load(3, half, 8 * 128))
            action(pltpu.make_async_copy(
                xsep_ref.at[:, pl.ds(COLS - COLS % 128, COLS % 128)], tail, load_sem.at[half, 4]))

    for half in (1, 0):
        for zone in range(3):
            load(zone, half, ZONES[zone][1] * 64).start()
        load_last(half, lambda copy: copy.start())
    loc_copy = pltpu.make_async_copy(xloc_ref, xl, loc_sem)
    loc_copy.start()

    row = lax.broadcasted_iota(jnp.int32, (16, 128), 0)
    lane = lax.broadcasted_iota(jnp.int32, (16, 128), 1)
    diagonal = row // 4 == lane // 32
    pick_rows = (lax.broadcasted_iota(jnp.int32, (16, 4), 0) % 4 == lax.broadcasted_iota(jnp.int32, (16, 4), 1))
    pick_lanes = (lax.broadcasted_iota(jnp.int32, (32, 128), 1) % 32 == lax.broadcasted_iota(jnp.int32, (32, 128), 0))
    rhs_copy.wait()
    sizes_copy.wait()
    tall = jnp.dot(pick_rows.astype(BF16), rhs_ref[...], preferred_element_type=F32).astype(BF16)
    wide = jnp.dot(tall, pick_lanes.astype(BF16), preferred_element_type=F32)
    rhs16 = jnp.where(diagonal, wide, 0.0).astype(BF16)

    def windows(zone, half):
        found = []
        for s in range(4):
            at = (BEGIN[zone] + window(zone, s) - ZONES[zone][0]) * 128
            found.append(xs[half, :, at : at + WIDE[zone] * 128])
        return jnp.concatenate(found, axis=0)

    def contributions(zone, half, store):
        product = jnp.dot(rhs16, windows(zone, half), preferred_element_type=F32)
        for j in range(WIDE[zone]):
            store[AT[zone] + j] = product[:, 128 * j : 128 * j + 128]

    def place_tail(half):
        @pl.when((core if half == 0 else 1 - core) == 1)
        def _():
            rest = jnp.concatenate([tail[...], jnp.zeros((32, 128 - tail.shape[1]), BF16)], axis=1)
            xs[half, :, TILES * 128 - 128 : TILES * 128] = rest

    def contribute(half, store):
        for zone in range(3):
            load(zone, half, ZONES[zone][1] * 64).wait()
            contributions(zone, half, store)
        load_last(half, lambda copy: copy.wait())
        place_tail(half)
        contributions(3, half, store)

    contribute(1, send_core)

    pl.semaphore_wait(barrier, greetings)
    for step in (2, -2):
        pl.semaphore_signal(token, inc=1, device_id=(along(step),), device_id_type=MESH)

    sibling = partner(CORE)
    core_copies = []
    for zone in range(4):
        blocks = pl.ds(AT[zone], WIDE[zone])
        copy = remote(send_core.at[blocks], recv_core.at[blocks], core_send.at[zone], core_recv.at[zone], sibling)
        copy.start()
        core_copies.append(copy)
    contribute(0, mine)

    def scatter(zone, count, owner, slot, landing, sem):
        for j in range(count):
            block = AT[zone] + j
            to = owner(j)

            @pl.when(to == me)
            def _():
                landing[slot] = mine[block]

            @pl.when(to != me)
            def _():
                remote(mine.at[block], landing.at[slot], rs_send.at[sem], rs_recv.at[sem], to).start()

    for zone in range(4):
        core_copies[zone].wait_recv()
        for j in range(WIDE[zone]):
            block = AT[zone] + j
            mine[block] = mine[block] + recv_core[block]
        if zone == 0:
            scatter(0, WIDE[0], owner_a, slot_a, recv_ab, 0)
        elif zone == 1:
            scatter(1, WIDE[1], owner_b, slot_b, recv_ab, 1)
        elif zone == 2:
            scatter(2, WIDE[2], owner_c, slot_c, recv_c, 2)

    def d_copy(n, mask):
        return remote(mine.at[pl.ds(AT[3], WIDE[3])], recv_d.at[n], rs_send.at[3 + n], rs_recv.at[3 + n], partner(mask))

    def d_do(action):
        for n, mask in enumerate(LINE):
            if mask & Z0:
                @pl.when(core == 0)
                def _():
                    action(d_copy(n, mask))
            else:
                action(d_copy(n, mask))

    def total(landing, count):
        acc = [landing[i] for i in range(4)]
        for i in range(4, count):
            acc[i % 4] = acc[i % 4] + landing[i]
        return (acc[0] + acc[1]) + (acc[2] + acc[3])

    def deep_copies(src, landing, at):
        return [
            remote(src, landing.at[m // Z1 - 1], z_send.at[at], z_recv.at[at], partner(m)) for m in DEPTH
        ]

    pl.semaphore_wait(token, 2)

    @pl.when(owns_a)
    def _():
        drain(recv_ab.at[pl.ds(0, 31)], rs_recv.at[0])
        part_ab[...] = total(recv_ab, 32)

    @pl.when(owns_b)
    def _():
        drain(recv_ab.at[pl.ds(0, 15)], rs_recv.at[1])
        part_ab[...] = total(recv_ab, 16)


    @pl.when(owns_ab)
    def _():
        for copy in deep_copies(part_ab, deep_ab, 0):
            copy.start()

    def c_far(action):
        for m in DEPTH_C:
            if m & Z3:
                @pl.when(core == 0)
                def _():
                    action(m)
            else:
                action(m)

    @pl.when(owns_c)
    def _():
        drain(recv_c.at[pl.ds(0, 15)], rs_recv.at[2])
        part_c[...] = total(recv_c, 16)
        c_far(lambda m: remote(
            part_c, deep_c.at[m // Z2 - 1], z_send.at[1], z_recv.at[1], partner(m)).start())

    d_do(lambda copy: copy.start())

    def active(columns, zone):
        lo, hi = ZONES[zone][0] * 128, sum(ZONES[zone]) * 128
        keep = None
        for level in range(9):
            if STARTS[level] < hi and ENDS[level] > lo:
                limit = STARTS[level] + sizes_ref[level]
                inside = jnp.logical_and(
                    jnp.logical_and(columns >= STARTS[level], columns < ENDS[level]), columns < limit)
                keep = inside if keep is None else jnp.logical_or(keep, inside)
        lo, hi = KEEP[zone]
        return jnp.logical_and(keep, jnp.logical_and(columns >= lo, columns < hi))

    def rounded(values, columns, end, zone):
        keep = jnp.logical_and(active(columns, zone), columns < end)
        return jnp.where(keep, values, 0.0).astype(BF16)

    d_do(lambda copy: copy.wait_recv())
    for j in range(WIDE[3]):
        columns, end = column_of(3, core, j)
        value = mine[AT[3] + j]
        for n, mask in enumerate(LINE):
            if mask & Z0:
                bound = jnp.where(core == 0, ENDS[5], 0)
            else:
                bound = ENDS[6] if mask & X1 else ENDS[7]
            value = value + jnp.where(columns < bound, recv_d[n, j], 0.0)
        full[0, AT[3] + j] = rounded(value, columns, end, 3)

    def relay(zone, at):
        blocks = pl.ds(AT[zone], WIDE[zone])
        return remote(full.at[0, blocks], full.at[1, blocks], relay_send.at[at], relay_recv.at[at], sibling)

    relay(3, 3).start()

    loc_copy.wait()
    x_loc = jnp.concatenate([xl[:, 1024 * s : 1024 * s + 1024] for s in range(4)], axis=0)
    interior = jnp.dot(rhs16, x_loc, preferred_element_type=F32).astype(BF16)
    contract = (((1,), (1,)), ((), ()))
    acc = lax.dot_general(interior, x_loc, contract, preferred_element_type=F32)

    def product(zone, half):
        blocks = jnp.concatenate([full[half, AT[zone] + j] for j in range(WIDE[zone])], axis=1)
        return lax.dot_general(blocks, windows(zone, half), contract, preferred_element_type=F32)

    def deep_total(part, landing):
        value = part[...]
        for i in range(7):
            value = value + landing[i]
        return value

    def gather(block, masks, sem):
        for mask in masks:
            remote(full.at[0, block], full.at[0, block], ag_send.at[sem], ag_recv.at[0, sem], partner(mask)).start()
            remote(full.at[0, block], full.at[1, block], ag_send.at[sem], ag_recv.at[1, sem], partner(mask | CORE)).start()
        remote(full.at[0, block], full.at[1, block], ag_send.at[sem], ag_recv.at[1, sem], partner(CORE)).start()

    @pl.when(owns_ab)
    def _():
        drain(deep_ab, z_recv.at[0])

    @pl.when(owns_a)
    def _():
        columns, end = column_of(0, core, a_mine)
        full[0, a_mine] = rounded(deep_total(part_ab, deep_ab), columns, end, 0)
        gather(a_mine, PLANE, 0)

    @pl.when(owns_b)
    def _():
        columns, end = column_of(1, core, k)
        full[0, AT[1] + k] = rounded(deep_total(part_ab, deep_ab), columns, end, 1)
        gather(AT[1] + k, PAIR, 1)

    @pl.when(owns_c)
    def _():
        @pl.when(core == 0)
        def _():
            drain(deep_c, z_recv.at[1])

        @pl.when(core == 1)
        def _():
            drain(deep_c.at[pl.ds(0, 1)], z_recv.at[1])

        columns, end = column_of(2, core, k)
        value = part_c[...]
        for m in range(1, 4):
            bound = ENDS[3] if m == 1 else jnp.where(core == 0, ENDS[2], 0)
            value = value + jnp.where(columns < bound, deep_c[m - 1], 0.0)
        full[0, AT[2] + k] = rounded(value, columns, end, 2)
        gather(AT[2] + k, SLAB, 2)

    acc = acc + product(3, 0)
    relay(3, 3).wait_recv()
    acc = acc + product(3, 1)

    for zone in range(4):
        core_copies[zone].wait_send()
    relay(3, 3).wait_send()

    def drain_scatter(owns, zone):
        @pl.when(owns)
        def _():
            drain(mine.at[pl.ds(0, WIDE[zone] - 1)], rs_send.at[zone])

        @pl.when(jnp.logical_not(owns))
        def _():
            drain(mine.at[pl.ds(0, WIDE[zone])], rs_send.at[zone])

    drain_scatter(owns_a, 0)
    drain_scatter(owns_b, 1)
    drain_scatter(owns_c, 2)
    d_do(lambda copy: copy.wait_send())

    @pl.when(owns_ab)
    def _():
        drain(deep_ab, z_send.at[0])

    @pl.when(jnp.logical_and(owns_c, core == 0))
    def _():
        drain(deep_c, z_send.at[1])

    @pl.when(jnp.logical_and(owns_c, core == 1))
    def _():
        drain(deep_c.at[pl.ds(0, 1)], z_send.at[1])

    def drain_gather(owns, zone):
        @pl.when(owns)
        def _():
            drain(full.at[0, pl.ds(AT[zone], WIDE[zone] - 1)], ag_recv.at[0, zone])

        @pl.when(jnp.logical_not(owns))
        def _():
            drain(full.at[0, pl.ds(AT[zone], WIDE[zone])], ag_recv.at[0, zone])

    def arrived(owns, zone):
        drain_gather(owns, zone)
        drain(full.at[1, pl.ds(AT[zone], WIDE[zone])], ag_recv.at[1, zone])
        return product(zone, 0) + product(zone, 1)

    acc = acc + arrived(owns_b, 1)
    acc = acc + arrived(owns_c, 2)
    acc = acc + arrived(owns_a, 0)
    out_ref[...] = (acc[0:4, 0:32] + acc[4:8, 32:64]) + (acc[8:12, 64:96] + acc[12:16, 96:128])

    @pl.when(owns_a)
    def _():
        drain(full, ag_send.at[0])
        drain(full.at[0, pl.ds(0, 1)], ag_send.at[0])

    @pl.when(owns_b)
    def _():
        drain(full.at[0, pl.ds(0, 31)], ag_send.at[1])

    @pl.when(owns_c)
    def _():
        drain(full.at[0, pl.ds(0, 31)], ag_send.at[2])


def body(rhs, x_sep, x_loc, sep_sizes):
    vmem, hbm = pl.BlockSpec(memory_space=pltpu.VMEM), pl.BlockSpec(memory_space=pltpu.HBM)
    dma = pltpu.SemaphoreType.DMA
    blocks = functools.partial(pltpu.VMEM, dtype=F32)
    return pl.pallas_call(
        kernel,
        out_shape=pltpu.VMEM((4, 32), F32),
        in_specs=[hbm] * 4,
        out_specs=vmem,
        scratch_shapes=[
            pltpu.VMEM((4, 32), BF16),
            pltpu.SMEM((9,), jnp.int32),
            pltpu.VMEM((2, 32, TILES * 128), BF16),
            pltpu.VMEM((32, COLS % 128), BF16),
            pltpu.VMEM((32, LOC), BF16),
            blocks((BLOCKS, 16, 128)),
            blocks((BLOCKS, 16, 128)),
            blocks((BLOCKS, 16, 128)),
            blocks((32, 16, 128)),
            blocks((16, 16, 128)),
            blocks((7, WIDE[3], 16, 128)),
            blocks((16, 128)),
            blocks((16, 128)),
            blocks((7, 16, 128)),
            blocks((3, 16, 128)),
            pltpu.VMEM((2, BLOCKS, 16, 128), BF16),
            dma((2,)),
            dma((2, 5)),
            dma,
            dma((4,)),
            dma((4,)),
            dma((10,)),
            dma((10,)),
            dma((2,)),
            dma((2,)),
            dma((3,)),
            dma((2, 3)),
            dma((4,)),
            dma((4,)),
            pltpu.SemaphoreType.REGULAR,
        ],
        compiler_params=pltpu.CompilerParams(
            collective_id=0, has_side_effects=True, vmem_limit_bytes=60 * 1024 * 1024
        ),
        name="xxt",
    )(rhs, sep_sizes, x_sep, x_loc)


def solution(mesh):
    placed = (P(None, "leaf"), P("leaf", None), P("leaf", None), P())
    return jax.shard_map(
        body, mesh=mesh, in_specs=placed, out_specs=P(None, "leaf"), check_vma=False
    )
```

```python
import functools

import jax
import jax.numpy as jnp
from jax import lax
from jax.experimental import pallas as pl
from jax.experimental.pallas import tpu as pltpu
from jax.sharding import PartitionSpec as P

MESH = pl.DeviceIdType.MESH
F32, BF16 = jnp.float32, jnp.bfloat16

CORE, X0, X1, Z0, Z1, Z2, Z3, Y0, Y1 = (1 << b for b in range(9))

ZONES = ((0, 100), (100, 50), (150, 64), (212, 18))
WIDE = (13, 7, 8, 3)
AT = (0, 13, 20, 28)
BLOCKS = 31
BEGIN = (0, 50, 75, 107)
TILES = 116
KEEP = ((0, 12800), (12800, 19200), (19200, 27200), (27200, 29400))
COLS = 29400
ENDS = (12800, 19200, 22400, 25600, 27200, 28000, 28800, 29200, 29400)
STARTS = (0,) + ENDS[:-1]
LOC = 4096


def window(zone, i):
    first, tiles = ZONES[zone]
    return first + (tiles * i) // 8


def column_of(zone, core, j):
    shape = (16, 128)
    i = 4 * core + lax.broadcasted_iota(jnp.int32, shape, 0) // 4
    lane = lax.broadcasted_iota(jnp.int32, shape, 1)
    first, tiles = ZONES[zone]
    start = first + (tiles * i) // 8
    end = first + (tiles * (i + 1)) // 8
    return (start + j) * 128 + lane, end * 128


def hops(mask):
    x, y, z = (mask // X0) % 4, (mask // Y0) % 4, (mask // Z0) % 4
    return (x > 0) + (x == 2) + (y > 0) + (y == 2) + z


def masks_of(bits):
    found = [0]
    for bit in bits:
        found += [m | bit for m in found]
    return sorted(found[1:], key=hops, reverse=True)


PLANE = masks_of((X0, X1, Z0, Y0, Y1))
PAIR = masks_of((X0, X1, Z0, Y0))
LINE = masks_of((X0, X1, Z0))
SLAB = masks_of((X0, X1, Z0, Z1))
DEPTH = [m * Z1 for m in (4, 5, 3, 6, 2, 7, 1)]
DEPTH_C = [m * Z1 for m in (4, 2, 6)]


def kernel(rhs_hbm, sizes_hbm, xsep_ref, xloc_ref, out_ref,
           rhs_ref, sizes_ref, xs, tail, xl, mine, send_core, recv_core, recv_ab, recv_c, recv_d, part_ab, part_c, deep_ab, deep_c, full,
           small_sem, load_sem, loc_sem, core_send, core_recv, rs_send, rs_recv, z_send, z_recv, ag_send, ag_recv,
           relay_send, relay_recv, token, near):
    me = lax.axis_index("leaf")

    def bit(b):
        return lax.rem(lax.div(me, jnp.int32(b)), jnp.int32(2))

    core = bit(CORE)
    y0, y1, z1 = bit(Y0), bit(Y1), bit(Z1)
    k = 4 * bit(X1) + 2 * bit(X0) + bit(Z0)
    turn = {b: 1 - 2 * bit(b) for b in (CORE, X0, X1, Z0, Z1, Z2, Z3, Y0, Y1)}
    delta = {b: turn[b] * b for b in turn}

    def partner(mask):
        other = me
        for b, d in delta.items():
            if mask & b:
                other = other + d
        return other

    def remote(src, dst, send, recv, device):
        return pltpu.make_async_remote_copy(
            src_ref=src, dst_ref=dst, send_sem=send, recv_sem=recv, device_id=(device,), device_id_type=MESH
        )

    def drain(ref, sem):
        pltpu.make_async_copy(ref, ref, sem).wait()

    role_a = y0 == core
    a_mine = 2 * k + y1
    owns_a = jnp.logical_and(role_a, a_mine < WIDE[0])
    owns_b = jnp.logical_and(jnp.logical_not(role_a), k < WIDE[1])
    slot_a = 16 * y1 + 8 * y0 + k
    slot_b = 8 * y0 + k
    slot_c = 8 * z1 + k
    owns_c = z1 == core
    owns_ab = jnp.logical_or(owns_a, owns_b)

    depth = lax.rem(lax.div(me, jnp.int32(Z1)), jnp.int32(8))

    def along(step):
        return me + (lax.rem(depth + (step + 8), jnp.int32(8)) - depth) * Z1

    barrier = pltpu.get_barrier_semaphore()
    sibling = partner(CORE)

    def greet(devices):
        for device in devices:
            pl.semaphore_signal(barrier, inc=1, device_id=(device - core,), device_id_type=MESH)

    def count(flag):
        return flag.astype(jnp.int32)

    @pl.when(core == 0)
    def _():
        pl.semaphore_signal(barrier, inc=1, device_id=(sibling,), device_id_type=MESH)

    @pl.when(owns_a)
    def _():
        greet(partner(m) for m in PLANE)

    @pl.when(owns_b)
    def _():
        greet(partner(m) for m in PAIR)

    @pl.when(owns_c)
    def _():
        greet(partner(m) for m in SLAB)

    @pl.when(jnp.logical_not(owns_ab))
    def _():
        greet(partner(m) for m in LINE)

    greet(along(s) for s in (2, -2, 1, -1))
    greetings = 0
    for c in (0, 1):
        takes_a = count(y0 == c)
        has_a = takes_a * count(a_mine < WIDE[0])
        has_b = (1 - takes_a) * count(k < WIDE[1])
        line_owners = 7 - takes_a * y1
        greetings += (
            (WIDE[0] - has_a) + (WIDE[1] - has_b) + (WIDE[2] - count(z1 == c)) + (8 - line_owners - (1 - has_a - has_b)) + 4
        )

    rhs_copy = pltpu.make_async_copy(rhs_hbm, rhs_ref, small_sem.at[0])
    sizes_copy = pltpu.make_async_copy(sizes_hbm, sizes_ref, small_sem.at[1])
    rhs_copy.start()
    sizes_copy.start()

    def load(zone, half, width):
        first, tiles = ZONES[zone]
        owner = core if half == 0 else 1 - core
        start = pl.multiple_of((first + owner * (tiles // 2)) * 128, 128)
        return pltpu.make_async_copy(
            xsep_ref.at[:, pl.ds(start, width)], xs.at[half, :, pl.ds(BEGIN[zone] * 128, width)],
            load_sem.at[half, zone])

    def load_last(half, action):
        @pl.when((core if half == 0 else 1 - core) == 0)
        def _():
            action(load(3, half, 9 * 128))

        @pl.when((core if half == 0 else 1 - core) == 1)
        def _():
            action(load(3, half, 8 * 128))
            action(pltpu.make_async_copy(
                xsep_ref.at[:, pl.ds(COLS - COLS % 128, COLS % 128)], tail, load_sem.at[half, 4]))

    for half in (1, 0):
        for zone in range(3):
            load(zone, half, ZONES[zone][1] * 64).start()
        load_last(half, lambda copy: copy.start())
    loc_copy = pltpu.make_async_copy(xloc_ref, xl, loc_sem)
    loc_copy.start()

    @pl.when(core == 1)
    def _():
        pl.semaphore_wait(barrier, 1)
        pl.semaphore_signal(near, inc=1, device_id=(sibling,), device_id_type=MESH)

    row = lax.broadcasted_iota(jnp.int32, (16, 128), 0)
    lane = lax.broadcasted_iota(jnp.int32, (16, 128), 1)
    diagonal = row // 4 == lane // 32
    pick_rows = (lax.broadcasted_iota(jnp.int32, (16, 4), 0) % 4 == lax.broadcasted_iota(jnp.int32, (16, 4), 1))
    pick_lanes = (lax.broadcasted_iota(jnp.int32, (32, 128), 1) % 32 == lax.broadcasted_iota(jnp.int32, (32, 128), 0))
    rhs_copy.wait()
    sizes_copy.wait()
    tall = jnp.dot(pick_rows.astype(BF16), rhs_ref[...], preferred_element_type=F32).astype(BF16)
    wide = jnp.dot(tall, pick_lanes.astype(BF16), preferred_element_type=F32)
    rhs16 = jnp.where(diagonal, wide, 0.0).astype(BF16)

    def windows(zone, half):
        found = []
        for s in range(4):
            at = (BEGIN[zone] + window(zone, s) - ZONES[zone][0]) * 128
            found.append(xs[half, :, at : at + WIDE[zone] * 128])
        return jnp.concatenate(found, axis=0)

    def contributions(zone, half, store):
        product = jnp.dot(rhs16, windows(zone, half), preferred_element_type=F32)
        for j in range(WIDE[zone]):
            store[AT[zone] + j] = product[:, 128 * j : 128 * j + 128]

    def place_tail(half):
        @pl.when((core if half == 0 else 1 - core) == 1)
        def _():
            rest = jnp.concatenate([tail[...], jnp.zeros((32, 128 - tail.shape[1]), BF16)], axis=1)
            xs[half, :, TILES * 128 - 128 : TILES * 128] = rest

    def contribute(half, store):
        for zone in range(3):
            load(zone, half, ZONES[zone][1] * 64).wait()
            contributions(zone, half, store)
        load_last(half, lambda copy: copy.wait())
        place_tail(half)
        contributions(3, half, store)

    contribute(1, send_core)

    @pl.when(core == 0)
    def _():
        pl.semaphore_wait(near, 1)

    core_copies = []
    for zone in range(4):
        blocks = pl.ds(AT[zone], WIDE[zone])
        copy = remote(send_core.at[blocks], recv_core.at[blocks], core_send.at[zone], core_recv.at[zone], sibling)
        copy.start()
        core_copies.append(copy)
    contribute(0, mine)

    @pl.when(core == 0)
    def _():
        pl.semaphore_wait(barrier, greetings)
        pl.semaphore_signal(near, inc=1, device_id=(sibling,), device_id_type=MESH)

    @pl.when(core == 1)
    def _():
        pl.semaphore_wait(near, 1)

    for step in (2, -2):
        pl.semaphore_signal(token, inc=1, device_id=(along(step),), device_id_type=MESH)

    def place(mask):
        return k + sum(turn[b] * w for b, w in ((X1, 4), (X0, 2), (Z0, 1)) if mask & b)

    def scatter(zone, masks, ahead, item, slot, landing):
        for mask in masks:
            to = partner(mask) + ahead
            j = item(mask)
            wanted = j < WIDE[zone]

            @pl.when(wanted if mask else jnp.logical_and(wanted, ahead != 0))
            def _():
                remote(mine.at[AT[zone] + j], landing.at[slot], rs_send.at[zone], rs_recv.at[zone], to).start()

    def scatter_a():
        scatter(0, masks_of((X0, X1, Z0, Y1)) + [0], (core - y0) * Y0,
                lambda m: 2 * place(m) + (y1 + turn[Y1] if m & Y1 else y1), slot_a, recv_ab)

        @pl.when(owns_a)
        def _():
            recv_ab[slot_a] = mine[a_mine]

    def scatter_b():
        scatter(1, LINE + [0], (1 - core - y0) * Y0, place, slot_b, recv_ab)

        @pl.when(owns_b)
        def _():
            recv_ab[slot_b] = mine[AT[1] + k]

    def scatter_c():
        scatter(2, LINE + [0], (core - z1) * Z1, place, slot_c, recv_c)

        @pl.when(owns_c)
        def _():
            recv_c[slot_c] = mine[AT[2] + k]

    for zone in range(4):
        core_copies[zone].wait_recv()
        for j in range(WIDE[zone]):
            block = AT[zone] + j
            mine[block] = mine[block] + recv_core[block]
        if zone < 3:
            (scatter_a, scatter_b, scatter_c)[zone]()

    def d_copy(n, mask):
        return remote(mine.at[pl.ds(AT[3], WIDE[3])], recv_d.at[n], rs_send.at[3 + n], rs_recv.at[3 + n], partner(mask))

    def d_do(action):
        for n, mask in enumerate(LINE):
            if mask & Z0:
                @pl.when(core == 0)
                def _():
                    action(d_copy(n, mask))
            else:
                action(d_copy(n, mask))

    def total(landing, count):
        acc = [landing[i] for i in range(4)]
        for i in range(4, count):
            acc[i % 4] = acc[i % 4] + landing[i]
        return (acc[0] + acc[1]) + (acc[2] + acc[3])

    def deep_copies(src, landing, at):
        return [
            remote(src, landing.at[m // Z1 - 1], z_send.at[at], z_recv.at[at], partner(m)) for m in DEPTH
        ]

    pl.semaphore_wait(token, 2)

    @pl.when(owns_a)
    def _():
        drain(recv_ab.at[pl.ds(0, 31)], rs_recv.at[0])
        part_ab[...] = total(recv_ab, 32)

    @pl.when(owns_b)
    def _():
        drain(recv_ab.at[pl.ds(0, 15)], rs_recv.at[1])
        part_ab[...] = total(recv_ab, 16)


    @pl.when(owns_ab)
    def _():
        for copy in deep_copies(part_ab, deep_ab, 0):
            copy.start()

    def c_far(action):
        for m in DEPTH_C:
            if m & Z3:
                @pl.when(core == 0)
                def _():
                    action(m)
            else:
                action(m)

    @pl.when(owns_c)
    def _():
        drain(recv_c.at[pl.ds(0, 15)], rs_recv.at[2])
        part_c[...] = total(recv_c, 16)
        c_far(lambda m: remote(
            part_c, deep_c.at[m // Z2 - 1], z_send.at[1], z_recv.at[1], partner(m)).start())

    d_do(lambda copy: copy.start())

    def active(columns, zone):
        lo, hi = ZONES[zone][0] * 128, sum(ZONES[zone]) * 128
        keep = None
        for level in range(9):
            if STARTS[level] < hi and ENDS[level] > lo:
                limit = STARTS[level] + sizes_ref[level]
                inside = jnp.logical_and(
                    jnp.logical_and(columns >= STARTS[level], columns < ENDS[level]), columns < limit)
                keep = inside if keep is None else jnp.logical_or(keep, inside)
        lo, hi = KEEP[zone]
        return jnp.logical_and(keep, jnp.logical_and(columns >= lo, columns < hi))

    def rounded(values, columns, end, zone):
        keep = jnp.logical_and(active(columns, zone), columns < end)
        return jnp.where(keep, values, 0.0).astype(BF16)

    d_do(lambda copy: copy.wait_recv())
    for j in range(WIDE[3]):
        columns, end = column_of(3, core, j)
        value = mine[AT[3] + j]
        for n, mask in enumerate(LINE):
            if mask & Z0:
                bound = jnp.where(core == 0, ENDS[5], 0)
            else:
                bound = ENDS[6] if mask & X1 else ENDS[7]
            value = value + jnp.where(columns < bound, recv_d[n, j], 0.0)
        full[0, AT[3] + j] = rounded(value, columns, end, 3)

    def relay(zone, at):
        blocks = pl.ds(AT[zone], WIDE[zone])
        return remote(full.at[0, blocks], full.at[1, blocks], relay_send.at[at], relay_recv.at[at], sibling)

    relay(3, 3).start()

    loc_copy.wait()
    x_loc = jnp.concatenate([xl[:, 1024 * s : 1024 * s + 1024] for s in range(4)], axis=0)
    interior = jnp.dot(rhs16, x_loc, preferred_element_type=F32).astype(BF16)
    contract = (((1,), (1,)), ((), ()))
    acc = lax.dot_general(interior, x_loc, contract, preferred_element_type=F32)

    def product(zone, half):
        blocks = jnp.concatenate([full[half, AT[zone] + j] for j in range(WIDE[zone])], axis=1)
        return lax.dot_general(blocks, windows(zone, half), contract, preferred_element_type=F32)

    def deep_total(part, landing):
        value = part[...]
        for i in range(7):
            value = value + landing[i]
        return value

    def gather(block, masks, sem):
        for mask in masks:
            remote(full.at[0, block], full.at[0, block], ag_send.at[sem], ag_recv.at[0, sem], partner(mask)).start()
            remote(full.at[0, block], full.at[1, block], ag_send.at[sem], ag_recv.at[1, sem], partner(mask | CORE)).start()
        remote(full.at[0, block], full.at[1, block], ag_send.at[sem], ag_recv.at[1, sem], partner(CORE)).start()

    @pl.when(owns_ab)
    def _():
        drain(deep_ab, z_recv.at[0])

    @pl.when(owns_a)
    def _():
        columns, end = column_of(0, core, a_mine)
        full[0, a_mine] = rounded(deep_total(part_ab, deep_ab), columns, end, 0)
        gather(a_mine, PLANE, 0)

    @pl.when(owns_b)
    def _():
        columns, end = column_of(1, core, k)
        full[0, AT[1] + k] = rounded(deep_total(part_ab, deep_ab), columns, end, 1)
        gather(AT[1] + k, PAIR, 1)

    @pl.when(owns_c)
    def _():
        @pl.when(core == 0)
        def _():
            drain(deep_c, z_recv.at[1])

        @pl.when(core == 1)
        def _():
            drain(deep_c.at[pl.ds(0, 1)], z_recv.at[1])

        columns, end = column_of(2, core, k)
        value = part_c[...]
        for m in range(1, 4):
            bound = ENDS[3] if m == 1 else jnp.where(core == 0, ENDS[2], 0)
            value = value + jnp.where(columns < bound, deep_c[m - 1], 0.0)
        full[0, AT[2] + k] = rounded(value, columns, end, 2)
        gather(AT[2] + k, SLAB, 2)

    acc = acc + product(3, 0)
    relay(3, 3).wait_recv()
    acc = acc + product(3, 1)

    for zone in range(4):
        core_copies[zone].wait_send()
    relay(3, 3).wait_send()

    def drain_scatter(owns, zone):
        @pl.when(owns)
        def _():
            drain(mine.at[pl.ds(0, WIDE[zone] - 1)], rs_send.at[zone])

        @pl.when(jnp.logical_not(owns))
        def _():
            drain(mine.at[pl.ds(0, WIDE[zone])], rs_send.at[zone])

    drain_scatter(owns_a, 0)
    drain_scatter(owns_b, 1)
    drain_scatter(owns_c, 2)
    d_do(lambda copy: copy.wait_send())

    @pl.when(owns_ab)
    def _():
        drain(deep_ab, z_send.at[0])

    @pl.when(jnp.logical_and(owns_c, core == 0))
    def _():
        drain(deep_c, z_send.at[1])

    @pl.when(jnp.logical_and(owns_c, core == 1))
    def _():
        drain(deep_c.at[pl.ds(0, 1)], z_send.at[1])

    def drain_gather(owns, zone):
        @pl.when(owns)
        def _():
            drain(full.at[0, pl.ds(AT[zone], WIDE[zone] - 1)], ag_recv.at[0, zone])

        @pl.when(jnp.logical_not(owns))
        def _():
            drain(full.at[0, pl.ds(AT[zone], WIDE[zone])], ag_recv.at[0, zone])

    def arrived(owns, zone):
        drain_gather(owns, zone)
        drain(full.at[1, pl.ds(AT[zone], WIDE[zone])], ag_recv.at[1, zone])
        return product(zone, 0) + product(zone, 1)

    acc = acc + arrived(owns_b, 1)
    acc = acc + arrived(owns_c, 2)
    acc = acc + arrived(owns_a, 0)
    out_ref[...] = (acc[0:4, 0:32] + acc[4:8, 32:64]) + (acc[8:12, 64:96] + acc[12:16, 96:128])

    @pl.when(owns_a)
    def _():
        drain(full, ag_send.at[0])
        drain(full.at[0, pl.ds(0, 1)], ag_send.at[0])

    @pl.when(owns_b)
    def _():
        drain(full.at[0, pl.ds(0, 31)], ag_send.at[1])

    @pl.when(owns_c)
    def _():
        drain(full.at[0, pl.ds(0, 31)], ag_send.at[2])


def body(rhs, x_sep, x_loc, sep_sizes):
    vmem, hbm = pl.BlockSpec(memory_space=pltpu.VMEM), pl.BlockSpec(memory_space=pltpu.HBM)
    dma = pltpu.SemaphoreType.DMA
    blocks = functools.partial(pltpu.VMEM, dtype=F32)
    return pl.pallas_call(
        kernel,
        out_shape=pltpu.VMEM((4, 32), F32),
        in_specs=[hbm] * 4,
        out_specs=vmem,
        scratch_shapes=[
            pltpu.VMEM((4, 32), BF16),
            pltpu.SMEM((9,), jnp.int32),
            pltpu.VMEM((2, 32, TILES * 128), BF16),
            pltpu.VMEM((32, COLS % 128), BF16),
            pltpu.VMEM((32, LOC), BF16),
            blocks((BLOCKS, 16, 128)),
            blocks((BLOCKS, 16, 128)),
            blocks((BLOCKS, 16, 128)),
            blocks((32, 16, 128)),
            blocks((16, 16, 128)),
            blocks((7, WIDE[3], 16, 128)),
            blocks((16, 128)),
            blocks((16, 128)),
            blocks((7, 16, 128)),
            blocks((3, 16, 128)),
            pltpu.VMEM((2, BLOCKS, 16, 128), BF16),
            dma((2,)),
            dma((2, 5)),
            dma,
            dma((4,)),
            dma((4,)),
            dma((10,)),
            dma((10,)),
            dma((2,)),
            dma((2,)),
            dma((3,)),
            dma((2, 3)),
            dma((4,)),
            dma((4,)),
            pltpu.SemaphoreType.REGULAR,
            pltpu.SemaphoreType.REGULAR,
        ],
        compiler_params=pltpu.CompilerParams(
            collective_id=0, has_side_effects=True, vmem_limit_bytes=60 * 1024 * 1024
        ),
        name="xxt",
    )(rhs, sep_sizes, x_sep, x_loc)


def solution(mesh):
    placed = (P(None, "leaf"), P("leaf", None), P("leaf", None), P())
    return jax.shard_map(
        body, mesh=mesh, in_specs=placed, out_specs=P(None, "leaf"), check_vma=False
    )
```

```python
import functools

import jax
import jax.numpy as jnp
from jax import lax
from jax.experimental import pallas as pl
from jax.experimental.pallas import tpu as pltpu
from jax.sharding import PartitionSpec as P

MESH = pl.DeviceIdType.MESH
F32, BF16 = jnp.float32, jnp.bfloat16

CORE, X0, X1, Z0, Z1, Z2, Z3, Y0, Y1 = (1 << b for b in range(9))

ZONES = ((0, 100), (100, 50), (150, 64), (212, 18))
WIDE = (13, 7, 8, 3)
AT = (0, 13, 20, 28)
BLOCKS = 31
BEGIN = (0, 50, 75, 107)
TILES = 116
KEEP = ((0, 12800), (12800, 19200), (19200, 27200), (27200, 29400))
COLS = 29400
ENDS = (12800, 19200, 22400, 25600, 27200, 28000, 28800, 29200, 29400)
STARTS = (0,) + ENDS[:-1]
LOC = 4096


def window(zone, i):
    first, tiles = ZONES[zone]
    return first + (tiles * i) // 8


def column_of(zone, core, j):
    shape = (16, 128)
    i = 4 * core + lax.broadcasted_iota(jnp.int32, shape, 0) // 4
    lane = lax.broadcasted_iota(jnp.int32, shape, 1)
    first, tiles = ZONES[zone]
    start = first + (tiles * i) // 8
    end = first + (tiles * (i + 1)) // 8
    return (start + j) * 128 + lane, end * 128


def hops(mask):
    x, y, z = (mask // X0) % 4, (mask // Y0) % 4, (mask // Z0) % 4
    return (x > 0) + (x == 2) + (y > 0) + (y == 2) + z


def masks_of(bits):
    found = [0]
    for bit in bits:
        found += [m | bit for m in found]
    return sorted(found[1:], key=hops, reverse=True)


PLANE = masks_of((X0, X1, Z0, Y0, Y1))
PAIR = masks_of((X0, X1, Z0, Y0))
LINE = masks_of((X0, X1, Z0))
SLAB = masks_of((X0, X1, Z0, Z1))
DEPTH = [m * Z1 for m in (4, 5, 3, 6, 2, 7, 1)]
DEPTH_C = [m * Z1 for m in (4, 2, 6)]


def kernel(rhs_hbm, sizes_hbm, xsep_ref, xloc_ref, out_ref,
           rhs_ref, sizes_ref, xs, tail, xl, mine, send_core, recv_core, recv_ab, recv_c, recv_d, part_ab, part_c, deep_ab, deep_c, full,
           small_sem, load_sem, loc_sem, core_send, core_recv, rs_send, rs_recv, z_send, z_recv, ag_send, ag_recv,
           relay_send, relay_recv, token, near):
    me = lax.axis_index("leaf")

    def bit(b):
        return lax.rem(lax.div(me, jnp.int32(b)), jnp.int32(2))

    core = bit(CORE)
    y0, y1, z1 = bit(Y0), bit(Y1), bit(Z1)
    k = 4 * bit(X1) + 2 * bit(X0) + bit(Z0)
    turn = {b: 1 - 2 * bit(b) for b in (CORE, X0, X1, Z0, Z1, Z2, Z3, Y0, Y1)}
    delta = {b: turn[b] * b for b in turn}

    def partner(mask):
        other = me
        for b, d in delta.items():
            if mask & b:
                other = other + d
        return other

    def remote(src, dst, send, recv, device):
        return pltpu.make_async_remote_copy(
            src_ref=src, dst_ref=dst, send_sem=send, recv_sem=recv, device_id=(device,), device_id_type=MESH
        )

    def drain(ref, sem):
        pltpu.make_async_copy(ref, ref, sem).wait()

    role_a = y0 == core
    a_mine = 2 * k + y1
    owns_a = jnp.logical_and(role_a, a_mine < WIDE[0])
    owns_b = jnp.logical_and(jnp.logical_not(role_a), k < WIDE[1])
    slot_a = 16 * y1 + 8 * y0 + k
    slot_b = 8 * y0 + k
    slot_c = 8 * z1 + k
    owns_c = z1 == core
    owns_ab = jnp.logical_or(owns_a, owns_b)

    depth = lax.rem(lax.div(me, jnp.int32(Z1)), jnp.int32(8))

    def along(step):
        return me + (lax.rem(depth + (step + 8), jnp.int32(8)) - depth) * Z1

    barrier = pltpu.get_barrier_semaphore()
    sibling = partner(CORE)

    def greet(devices):
        for device in devices:
            pl.semaphore_signal(barrier, inc=1, device_id=(device - core,), device_id_type=MESH)

    def count(flag):
        return flag.astype(jnp.int32)

    @pl.when(core == 0)
    def _():
        pl.semaphore_signal(barrier, inc=1, device_id=(sibling,), device_id_type=MESH)

    @pl.when(owns_a)
    def _():
        greet(partner(m) for m in PLANE)

    @pl.when(owns_b)
    def _():
        greet(partner(m) for m in PAIR)

    @pl.when(owns_c)
    def _():
        greet(partner(m) for m in SLAB)

    @pl.when(jnp.logical_not(owns_ab))
    def _():
        greet(partner(m) for m in LINE)

    greet(along(s) for s in (2, -2, 1, -1))
    greetings = 0
    for c in (0, 1):
        takes_a = count(y0 == c)
        has_a = takes_a * count(a_mine < WIDE[0])
        has_b = (1 - takes_a) * count(k < WIDE[1])
        line_owners = 7 - takes_a * y1
        greetings += (
            (WIDE[0] - has_a) + (WIDE[1] - has_b) + (WIDE[2] - count(z1 == c)) + (8 - line_owners - (1 - has_a - has_b)) + 4
        )

    rhs_copy = pltpu.make_async_copy(rhs_hbm, rhs_ref, small_sem.at[0])
    sizes_copy = pltpu.make_async_copy(sizes_hbm, sizes_ref, small_sem.at[1])
    rhs_copy.start()
    sizes_copy.start()

    def load(zone, half, width):
        first, tiles = ZONES[zone]
        owner = core if half == 0 else 1 - core
        start = pl.multiple_of((first + owner * (tiles // 2)) * 128, 128)
        return pltpu.make_async_copy(
            xsep_ref.at[:, pl.ds(start, width)], xs.at[half, :, pl.ds(BEGIN[zone] * 128, width)],
            load_sem.at[half, zone])

    def load_last(half, action):
        @pl.when((core if half == 0 else 1 - core) == 0)
        def _():
            action(load(3, half, 9 * 128))

        @pl.when((core if half == 0 else 1 - core) == 1)
        def _():
            action(load(3, half, 8 * 128))
            action(pltpu.make_async_copy(
                xsep_ref.at[:, pl.ds(COLS - COLS % 128, COLS % 128)], tail, load_sem.at[half, 4]))

    for half in (1, 0):
        for zone in range(3):
            load(zone, half, ZONES[zone][1] * 64).start()
        load_last(half, lambda copy: copy.start())
    loc_copy = pltpu.make_async_copy(xloc_ref, xl, loc_sem)
    loc_copy.start()

    @pl.when(core == 1)
    def _():
        pl.semaphore_wait(barrier, 1)
        pl.semaphore_signal(near, inc=1, device_id=(sibling,), device_id_type=MESH)

    row = lax.broadcasted_iota(jnp.int32, (16, 128), 0)
    lane = lax.broadcasted_iota(jnp.int32, (16, 128), 1)
    diagonal = row // 4 == lane // 32
    pick_rows = (lax.broadcasted_iota(jnp.int32, (16, 4), 0) % 4 == lax.broadcasted_iota(jnp.int32, (16, 4), 1))
    pick_lanes = (lax.broadcasted_iota(jnp.int32, (32, 128), 1) % 32 == lax.broadcasted_iota(jnp.int32, (32, 128), 0))
    rhs_copy.wait()
    sizes_copy.wait()
    tall = jnp.dot(pick_rows.astype(BF16), rhs_ref[...], preferred_element_type=F32).astype(BF16)
    wide = jnp.dot(tall, pick_lanes.astype(BF16), preferred_element_type=F32)
    rhs16 = jnp.where(diagonal, wide, 0.0).astype(BF16)

    def windows(zone, half):
        found = []
        for s in range(4):
            at = (BEGIN[zone] + window(zone, s) - ZONES[zone][0]) * 128
            found.append(xs[half, :, at : at + WIDE[zone] * 128])
        return jnp.concatenate(found, axis=0)

    def contributions(zone, half, store):
        product = jnp.dot(rhs16, windows(zone, half), preferred_element_type=F32)
        for j in range(WIDE[zone]):
            store[AT[zone] + j] = product[:, 128 * j : 128 * j + 128]

    def place_tail(half):
        @pl.when((core if half == 0 else 1 - core) == 1)
        def _():
            rest = jnp.concatenate([tail[...], jnp.zeros((32, 128 - tail.shape[1]), BF16)], axis=1)
            xs[half, :, TILES * 128 - 128 : TILES * 128] = rest

    def contribute(zone, half, store):
        if zone < 3:
            load(zone, half, ZONES[zone][1] * 64).wait()
        else:
            load_last(half, lambda copy: copy.wait())
            place_tail(half)
        contributions(zone, half, store)

    @pl.when(core == 0)
    def _():
        pl.semaphore_wait(near, 1)

    core_copies = []
    for zone in range(4):
        contribute(zone, 1, send_core)
        blocks = pl.ds(AT[zone], WIDE[zone])
        copy = remote(send_core.at[blocks], recv_core.at[blocks], core_send.at[zone], core_recv.at[zone], sibling)
        copy.start()
        core_copies.append(copy)
    for zone in range(4):
        contribute(zone, 0, mine)

    @pl.when(core == 0)
    def _():
        pl.semaphore_wait(barrier, greetings)
        pl.semaphore_signal(near, inc=1, device_id=(sibling,), device_id_type=MESH)

    @pl.when(core == 1)
    def _():
        pl.semaphore_wait(near, 1)

    for step in (2, -2):
        pl.semaphore_signal(token, inc=1, device_id=(along(step),), device_id_type=MESH)

    def place(mask):
        return k + sum(turn[b] * w for b, w in ((X1, 4), (X0, 2), (Z0, 1)) if mask & b)

    def scatter(zone, masks, ahead, item, slot, landing):
        for mask in masks:
            to = partner(mask) + ahead
            j = item(mask)
            wanted = j < WIDE[zone]

            @pl.when(wanted if mask else jnp.logical_and(wanted, ahead != 0))
            def _():
                remote(mine.at[AT[zone] + j], landing.at[slot], rs_send.at[zone], rs_recv.at[zone], to).start()

    def scatter_a():
        scatter(0, masks_of((X0, X1, Z0, Y1)) + [0], (core - y0) * Y0,
                lambda m: 2 * place(m) + (y1 + turn[Y1] if m & Y1 else y1), slot_a, recv_ab)

        @pl.when(owns_a)
        def _():
            recv_ab[slot_a] = mine[a_mine]

    def scatter_b():
        scatter(1, LINE + [0], (1 - core - y0) * Y0, place, slot_b, recv_ab)

        @pl.when(owns_b)
        def _():
            recv_ab[slot_b] = mine[AT[1] + k]

    def scatter_c():
        scatter(2, LINE + [0], (core - z1) * Z1, place, slot_c, recv_c)

        @pl.when(owns_c)
        def _():
            recv_c[slot_c] = mine[AT[2] + k]

    for zone in range(4):
        core_copies[zone].wait_recv()
        for j in range(WIDE[zone]):
            block = AT[zone] + j
            mine[block] = mine[block] + recv_core[block]
        if zone < 3:
            (scatter_a, scatter_b, scatter_c)[zone]()

    def d_copy(n, mask):
        return remote(mine.at[pl.ds(AT[3], WIDE[3])], recv_d.at[n], rs_send.at[3 + n], rs_recv.at[3 + n], partner(mask))

    def d_do(action):
        for n, mask in enumerate(LINE):
            if mask & Z0:
                @pl.when(core == 0)
                def _():
                    action(d_copy(n, mask))
            else:
                action(d_copy(n, mask))

    def total(landing, count):
        acc = [landing[i] for i in range(4)]
        for i in range(4, count):
            acc[i % 4] = acc[i % 4] + landing[i]
        return (acc[0] + acc[1]) + (acc[2] + acc[3])

    def deep_copies(src, landing, at):
        return [
            remote(src, landing.at[m // Z1 - 1], z_send.at[at], z_recv.at[at], partner(m)) for m in DEPTH
        ]

    pl.semaphore_wait(token, 2)

    @pl.when(owns_a)
    def _():
        drain(recv_ab.at[pl.ds(0, 31)], rs_recv.at[0])
        part_ab[...] = total(recv_ab, 32)

    @pl.when(owns_b)
    def _():
        drain(recv_ab.at[pl.ds(0, 15)], rs_recv.at[1])
        part_ab[...] = total(recv_ab, 16)


    @pl.when(owns_ab)
    def _():
        for copy in deep_copies(part_ab, deep_ab, 0):
            copy.start()

    def c_far(action):
        for m in DEPTH_C:
            if m & Z3:
                @pl.when(core == 0)
                def _():
                    action(m)
            else:
                action(m)

    @pl.when(owns_c)
    def _():
        drain(recv_c.at[pl.ds(0, 15)], rs_recv.at[2])
        part_c[...] = total(recv_c, 16)
        c_far(lambda m: remote(
            part_c, deep_c.at[m // Z2 - 1], z_send.at[1], z_recv.at[1], partner(m)).start())

    d_do(lambda copy: copy.start())

    def active(columns, zone):
        lo, hi = ZONES[zone][0] * 128, sum(ZONES[zone]) * 128
        keep = None
        for level in range(9):
            if STARTS[level] < hi and ENDS[level] > lo:
                limit = STARTS[level] + sizes_ref[level]
                inside = jnp.logical_and(
                    jnp.logical_and(columns >= STARTS[level], columns < ENDS[level]), columns < limit)
                keep = inside if keep is None else jnp.logical_or(keep, inside)
        lo, hi = KEEP[zone]
        return jnp.logical_and(keep, jnp.logical_and(columns >= lo, columns < hi))

    def rounded(values, columns, end, zone):
        keep = jnp.logical_and(active(columns, zone), columns < end)
        return jnp.where(keep, values, 0.0).astype(BF16)

    d_do(lambda copy: copy.wait_recv())
    for j in range(WIDE[3]):
        columns, end = column_of(3, core, j)
        value = mine[AT[3] + j]
        for n, mask in enumerate(LINE):
            if mask & Z0:
                bound = jnp.where(core == 0, ENDS[5], 0)
            else:
                bound = ENDS[6] if mask & X1 else ENDS[7]
            value = value + jnp.where(columns < bound, recv_d[n, j], 0.0)
        full[0, AT[3] + j] = rounded(value, columns, end, 3)

    def relay(zone, at):
        blocks = pl.ds(AT[zone], WIDE[zone])
        return remote(full.at[0, blocks], full.at[1, blocks], relay_send.at[at], relay_recv.at[at], sibling)

    relay(3, 3).start()

    loc_copy.wait()
    x_loc = jnp.concatenate([xl[:, 1024 * s : 1024 * s + 1024] for s in range(4)], axis=0)
    interior = jnp.dot(rhs16, x_loc, preferred_element_type=F32).astype(BF16)
    contract = (((1,), (1,)), ((), ()))
    acc = lax.dot_general(interior, x_loc, contract, preferred_element_type=F32)

    def product(zone, half):
        blocks = jnp.concatenate([full[half, AT[zone] + j] for j in range(WIDE[zone])], axis=1)
        return lax.dot_general(blocks, windows(zone, half), contract, preferred_element_type=F32)

    def deep_total(part, landing):
        value = part[...]
        for i in range(7):
            value = value + landing[i]
        return value

    def gather(block, masks, sem):
        for mask in masks:
            remote(full.at[0, block], full.at[0, block], ag_send.at[sem], ag_recv.at[0, sem], partner(mask)).start()
            remote(full.at[0, block], full.at[1, block], ag_send.at[sem], ag_recv.at[1, sem], partner(mask | CORE)).start()
        remote(full.at[0, block], full.at[1, block], ag_send.at[sem], ag_recv.at[1, sem], partner(CORE)).start()

    @pl.when(owns_ab)
    def _():
        drain(deep_ab, z_recv.at[0])

    @pl.when(owns_a)
    def _():
        columns, end = column_of(0, core, a_mine)
        full[0, a_mine] = rounded(deep_total(part_ab, deep_ab), columns, end, 0)
        gather(a_mine, PLANE, 0)

    @pl.when(owns_b)
    def _():
        columns, end = column_of(1, core, k)
        full[0, AT[1] + k] = rounded(deep_total(part_ab, deep_ab), columns, end, 1)
        gather(AT[1] + k, PAIR, 1)

    @pl.when(owns_c)
    def _():
        @pl.when(core == 0)
        def _():
            drain(deep_c, z_recv.at[1])

        @pl.when(core == 1)
        def _():
            drain(deep_c.at[pl.ds(0, 1)], z_recv.at[1])

        columns, end = column_of(2, core, k)
        value = part_c[...]
        for m in range(1, 4):
            bound = ENDS[3] if m == 1 else jnp.where(core == 0, ENDS[2], 0)
            value = value + jnp.where(columns < bound, deep_c[m - 1], 0.0)
        full[0, AT[2] + k] = rounded(value, columns, end, 2)
        gather(AT[2] + k, SLAB, 2)

    acc = acc + product(3, 0)
    relay(3, 3).wait_recv()
    acc = acc + product(3, 1)

    for zone in range(4):
        core_copies[zone].wait_send()
    relay(3, 3).wait_send()

    def drain_scatter(owns, zone):
        @pl.when(owns)
        def _():
            drain(mine.at[pl.ds(0, WIDE[zone] - 1)], rs_send.at[zone])

        @pl.when(jnp.logical_not(owns))
        def _():
            drain(mine.at[pl.ds(0, WIDE[zone])], rs_send.at[zone])

    drain_scatter(owns_a, 0)
    drain_scatter(owns_b, 1)
    drain_scatter(owns_c, 2)
    d_do(lambda copy: copy.wait_send())

    @pl.when(owns_ab)
    def _():
        drain(deep_ab, z_send.at[0])

    @pl.when(jnp.logical_and(owns_c, core == 0))
    def _():
        drain(deep_c, z_send.at[1])

    @pl.when(jnp.logical_and(owns_c, core == 1))
    def _():
        drain(deep_c.at[pl.ds(0, 1)], z_send.at[1])

    def drain_gather(owns, zone):
        @pl.when(owns)
        def _():
            drain(full.at[0, pl.ds(AT[zone], WIDE[zone] - 1)], ag_recv.at[0, zone])

        @pl.when(jnp.logical_not(owns))
        def _():
            drain(full.at[0, pl.ds(AT[zone], WIDE[zone])], ag_recv.at[0, zone])

    def arrived(owns, zone):
        drain_gather(owns, zone)
        drain(full.at[1, pl.ds(AT[zone], WIDE[zone])], ag_recv.at[1, zone])
        return product(zone, 0) + product(zone, 1)

    acc = acc + arrived(owns_b, 1)
    acc = acc + arrived(owns_a, 0)
    acc = acc + arrived(owns_c, 2)
    out_ref[...] = (acc[0:4, 0:32] + acc[4:8, 32:64]) + (acc[8:12, 64:96] + acc[12:16, 96:128])

    @pl.when(owns_a)
    def _():
        drain(full, ag_send.at[0])
        drain(full.at[0, pl.ds(0, 1)], ag_send.at[0])

    @pl.when(owns_b)
    def _():
        drain(full.at[0, pl.ds(0, 31)], ag_send.at[1])

    @pl.when(owns_c)
    def _():
        drain(full.at[0, pl.ds(0, 31)], ag_send.at[2])


def body(rhs, x_sep, x_loc, sep_sizes):
    vmem, hbm = pl.BlockSpec(memory_space=pltpu.VMEM), pl.BlockSpec(memory_space=pltpu.HBM)
    dma = pltpu.SemaphoreType.DMA
    blocks = functools.partial(pltpu.VMEM, dtype=F32)
    return pl.pallas_call(
        kernel,
        out_shape=pltpu.VMEM((4, 32), F32),
        in_specs=[hbm] * 4,
        out_specs=vmem,
        scratch_shapes=[
            pltpu.VMEM((4, 32), BF16),
            pltpu.SMEM((9,), jnp.int32),
            pltpu.VMEM((2, 32, TILES * 128), BF16),
            pltpu.VMEM((32, COLS % 128), BF16),
            pltpu.VMEM((32, LOC), BF16),
            blocks((BLOCKS, 16, 128)),
            blocks((BLOCKS, 16, 128)),
            blocks((BLOCKS, 16, 128)),
            blocks((32, 16, 128)),
            blocks((16, 16, 128)),
            blocks((7, WIDE[3], 16, 128)),
            blocks((16, 128)),
            blocks((16, 128)),
            blocks((7, 16, 128)),
            blocks((3, 16, 128)),
            pltpu.VMEM((2, BLOCKS, 16, 128), BF16),
            dma((2,)),
            dma((2, 5)),
            dma,
            dma((4,)),
            dma((4,)),
            dma((10,)),
            dma((10,)),
            dma((2,)),
            dma((2,)),
            dma((3,)),
            dma((2, 3)),
            dma((4,)),
            dma((4,)),
            pltpu.SemaphoreType.REGULAR,
            pltpu.SemaphoreType.REGULAR,
        ],
        compiler_params=pltpu.CompilerParams(
            collective_id=0, has_side_effects=True, vmem_limit_bytes=60 * 1024 * 1024
        ),
        name="xxt",
    )(rhs, sep_sizes, x_sep, x_loc)


def solution(mesh):
    placed = (P(None, "leaf"), P("leaf", None), P("leaf", None), P())
    return jax.shard_map(
        body, mesh=mesh, in_specs=placed, out_specs=P(None, "leaf"), check_vma=False
    )
```

```python
import functools

import jax
import jax.numpy as jnp
from jax import lax
from jax.experimental import pallas as pl
from jax.experimental.pallas import tpu as pltpu
from jax.sharding import PartitionSpec as P

MESH = pl.DeviceIdType.MESH
F32, BF16 = jnp.float32, jnp.bfloat16

CORE, X0, X1, Z0, Z1, Z2, Z3, Y0, Y1 = (1 << b for b in range(9))

ZONES = ((0, 100), (100, 50), (150, 64), (212, 18))
WIDE = (13, 7, 8, 3)
AT = (0, 13, 20, 28)
BLOCKS = 31
BEGIN = (0, 50, 75, 107)
TILES = 116
KEEP = ((0, 12800), (12800, 19200), (19200, 27200), (27200, 29400))
COLS = 29400
ENDS = (12800, 19200, 22400, 25600, 27200, 28000, 28800, 29200, 29400)
STARTS = (0,) + ENDS[:-1]
LOC = 4096


def window(zone, i):
    first, tiles = ZONES[zone]
    return first + (tiles * i) // 8


def column_of(zone, core, j):
    shape = (16, 128)
    i = 4 * core + lax.broadcasted_iota(jnp.int32, shape, 0) // 4
    lane = lax.broadcasted_iota(jnp.int32, shape, 1)
    first, tiles = ZONES[zone]
    start = first + (tiles * i) // 8
    end = first + (tiles * (i + 1)) // 8
    return (start + j) * 128 + lane, end * 128


def hops(mask):
    x, y, z = (mask // X0) % 4, (mask // Y0) % 4, (mask // Z0) % 4
    return (x > 0) + (x == 2) + (y > 0) + (y == 2) + z


def masks_of(bits):
    found = [0]
    for bit in bits:
        found += [m | bit for m in found]
    return sorted(found[1:], key=hops, reverse=True)


PLANE = masks_of((X0, X1, Z0, Y0, Y1))
PAIR = masks_of((X0, X1, Z0, Y0))
LINE = masks_of((X0, X1, Z0))
DEPTH = [m * Z1 for m in (4, 5, 3, 6, 2, 7, 1)]


def kernel(rhs_hbm, sizes_hbm, xsep_ref, xloc_ref, out_ref,
           rhs_ref, sizes_ref, xs, tail, xl, mine, send_core, recv_core, recv_ab, recv_c, recv_d, part_ab, part_c, deep_ab, deep_c, full,
           small_sem, load_sem, loc_sem, core_send, core_recv, rs_send, rs_recv, z_send, z_recv, ag_send, ag_recv,
           relay_send, relay_recv, token, near):
    me = lax.axis_index("leaf")

    def bit(b):
        return lax.rem(lax.div(me, jnp.int32(b)), jnp.int32(2))

    core = bit(CORE)
    y0, y1, z1 = bit(Y0), bit(Y1), bit(Z1)
    k = 4 * bit(X1) + 2 * bit(X0) + bit(Z0)
    turn = {b: 1 - 2 * bit(b) for b in (CORE, X0, X1, Z0, Z1, Z2, Z3, Y0, Y1)}
    delta = {b: turn[b] * b for b in turn}

    def partner(mask):
        other = me
        for b, d in delta.items():
            if mask & b:
                other = other + d
        return other

    def remote(src, dst, send, recv, device):
        return pltpu.make_async_remote_copy(
            src_ref=src, dst_ref=dst, send_sem=send, recv_sem=recv, device_id=(device,), device_id_type=MESH
        )

    def drain(ref, sem):
        pltpu.make_async_copy(ref, ref, sem).wait()

    role_a = y0 == core
    a_mine = 2 * k + y1
    owns_a = jnp.logical_and(role_a, a_mine < WIDE[0])
    owns_b = jnp.logical_and(jnp.logical_not(role_a), k < WIDE[1])
    slot_a = 16 * y1 + 8 * y0 + k
    slot_b = 8 * y0 + k
    owns_ab = jnp.logical_or(owns_a, owns_b)

    depth = lax.rem(lax.div(me, jnp.int32(Z1)), jnp.int32(8))

    def along(step):
        return me + (lax.rem(depth + (step + 8), jnp.int32(8)) - depth) * Z1

    barrier = pltpu.get_barrier_semaphore()
    sibling = partner(CORE)

    def greet(devices):
        for device in devices:
            pl.semaphore_signal(barrier, inc=1, device_id=(device - core,), device_id_type=MESH)

    def count(flag):
        return flag.astype(jnp.int32)

    @pl.when(core == 0)
    def _():
        pl.semaphore_signal(barrier, inc=1, device_id=(sibling,), device_id_type=MESH)

    @pl.when(owns_a)
    def _():
        greet(partner(m) for m in PLANE)

    @pl.when(owns_b)
    def _():
        greet(partner(m) for m in PAIR)

    @pl.when(jnp.logical_not(owns_ab))
    def _():
        greet(partner(m) for m in LINE)

    greet(along(s) for s in (2, -2, 1, -1))
    greetings = 0
    for c in (0, 1):
        takes_a = count(y0 == c)
        has_a = takes_a * count(a_mine < WIDE[0])
        has_b = (1 - takes_a) * count(k < WIDE[1])
        line_owners = 7 - takes_a * y1
        greetings += (
            (WIDE[0] - has_a) + (WIDE[1] - has_b) + (8 - line_owners - (1 - has_a - has_b)) + 4
        )

    rhs_copy = pltpu.make_async_copy(rhs_hbm, rhs_ref, small_sem.at[0])
    sizes_copy = pltpu.make_async_copy(sizes_hbm, sizes_ref, small_sem.at[1])
    rhs_copy.start()
    sizes_copy.start()

    def load(zone, half, width):
        first, tiles = ZONES[zone]
        owner = core if half == 0 else 1 - core
        start = pl.multiple_of((first + owner * (tiles // 2)) * 128, 128)
        return pltpu.make_async_copy(
            xsep_ref.at[:, pl.ds(start, width)], xs.at[half, :, pl.ds(BEGIN[zone] * 128, width)],
            load_sem.at[half, zone])

    def load_last(half, action):
        @pl.when((core if half == 0 else 1 - core) == 0)
        def _():
            action(load(3, half, 9 * 128))

        @pl.when((core if half == 0 else 1 - core) == 1)
        def _():
            action(load(3, half, 8 * 128))
            action(pltpu.make_async_copy(
                xsep_ref.at[:, pl.ds(COLS - COLS % 128, COLS % 128)], tail, load_sem.at[half, 4]))

    for half in (1, 0):
        for zone in range(3):
            load(zone, half, ZONES[zone][1] * 64).start()
        load_last(half, lambda copy: copy.start())
    loc_copy = pltpu.make_async_copy(xloc_ref, xl, loc_sem)
    loc_copy.start()

    @pl.when(core == 1)
    def _():
        pl.semaphore_wait(barrier, 1)
        pl.semaphore_signal(near, inc=1, device_id=(sibling,), device_id_type=MESH)

    row = lax.broadcasted_iota(jnp.int32, (16, 128), 0)
    lane = lax.broadcasted_iota(jnp.int32, (16, 128), 1)
    diagonal = row // 4 == lane // 32
    pick_rows = (lax.broadcasted_iota(jnp.int32, (16, 4), 0) % 4 == lax.broadcasted_iota(jnp.int32, (16, 4), 1))
    pick_lanes = (lax.broadcasted_iota(jnp.int32, (32, 128), 1) % 32 == lax.broadcasted_iota(jnp.int32, (32, 128), 0))
    rhs_copy.wait()
    sizes_copy.wait()
    tall = jnp.dot(pick_rows.astype(BF16), rhs_ref[...], preferred_element_type=F32).astype(BF16)
    wide = jnp.dot(tall, pick_lanes.astype(BF16), preferred_element_type=F32)
    rhs16 = jnp.where(diagonal, wide, 0.0).astype(BF16)

    def windows(zone, half):
        found = []
        for s in range(4):
            at = (BEGIN[zone] + window(zone, s) - ZONES[zone][0]) * 128
            found.append(xs[half, :, at : at + WIDE[zone] * 128])
        return jnp.concatenate(found, axis=0)

    def contributions(zone, half, store):
        product = jnp.dot(rhs16, windows(zone, half), preferred_element_type=F32)
        for j in range(WIDE[zone]):
            store[AT[zone] + j] = product[:, 128 * j : 128 * j + 128]

    def place_tail(half):
        @pl.when((core if half == 0 else 1 - core) == 1)
        def _():
            rest = jnp.concatenate([tail[...], jnp.zeros((32, 128 - tail.shape[1]), BF16)], axis=1)
            xs[half, :, TILES * 128 - 128 : TILES * 128] = rest

    def contribute(zone, half, store):
        if zone < 3:
            load(zone, half, ZONES[zone][1] * 64).wait()
        else:
            load_last(half, lambda copy: copy.wait())
            place_tail(half)
        contributions(zone, half, store)

    @pl.when(core == 0)
    def _():
        pl.semaphore_wait(near, 1)

    core_copies = []
    for zone in range(4):
        contribute(zone, 1, send_core)
        blocks = pl.ds(AT[zone], WIDE[zone])
        copy = remote(send_core.at[blocks], recv_core.at[blocks], core_send.at[zone], core_recv.at[zone], sibling)
        copy.start()
        core_copies.append(copy)
    for zone in range(4):
        contribute(zone, 0, mine)

    @pl.when(core == 0)
    def _():
        pl.semaphore_wait(barrier, greetings)
        pl.semaphore_signal(near, inc=1, device_id=(sibling,), device_id_type=MESH)

    @pl.when(core == 1)
    def _():
        pl.semaphore_wait(near, 1)

    for step in (2, -2):
        pl.semaphore_signal(token, inc=1, device_id=(along(step),), device_id_type=MESH)

    def place(mask):
        return k + sum(turn[b] * w for b, w in ((X1, 4), (X0, 2), (Z0, 1)) if mask & b)

    def scatter(zone, masks, ahead, item, slot, landing):
        for mask in masks:
            to = partner(mask) + ahead
            j = item(mask)
            wanted = j < WIDE[zone]

            @pl.when(wanted if mask else jnp.logical_and(wanted, ahead != 0))
            def _():
                remote(mine.at[AT[zone] + j], landing.at[slot], rs_send.at[zone], rs_recv.at[zone], to).start()

    def scatter_a():
        scatter(0, masks_of((X0, X1, Z0, Y1)) + [0], (core - y0) * Y0,
                lambda m: 2 * place(m) + (y1 + turn[Y1] if m & Y1 else y1), slot_a, recv_ab)

        @pl.when(owns_a)
        def _():
            recv_ab[slot_a] = mine[a_mine]

    def scatter_b():
        scatter(1, LINE + [0], (1 - core - y0) * Y0, place, slot_b, recv_ab)

        @pl.when(owns_b)
        def _():
            recv_ab[slot_b] = mine[AT[1] + k]

    def scatter_c():
        scatter(2, LINE, 0, place, k, recv_c)
        recv_c[k] = mine[AT[2] + k]

    for zone in range(4):
        core_copies[zone].wait_recv()
        for j in range(WIDE[zone]):
            block = AT[zone] + j
            mine[block] = mine[block] + recv_core[block]
        if zone < 3:
            (scatter_a, scatter_b, scatter_c)[zone]()

    def d_copy(n, mask):
        return remote(mine.at[pl.ds(AT[3], WIDE[3])], recv_d.at[n], rs_send.at[3 + n], rs_recv.at[3 + n], partner(mask))

    def d_do(action):
        for n, mask in enumerate(LINE):
            if mask & Z0:
                @pl.when(core == 0)
                def _():
                    action(d_copy(n, mask))
            else:
                action(d_copy(n, mask))

    def total(landing, count):
        acc = [landing[i] for i in range(4)]
        for i in range(4, count):
            acc[i % 4] = acc[i % 4] + landing[i]
        return (acc[0] + acc[1]) + (acc[2] + acc[3])

    def deep_copies(src, landing, at):
        return [
            remote(src, landing.at[m // Z1 - 1], z_send.at[at], z_recv.at[at], partner(m)) for m in DEPTH
        ]

    pl.semaphore_wait(token, 2)

    @pl.when(owns_a)
    def _():
        drain(recv_ab.at[pl.ds(0, 31)], rs_recv.at[0])
        part_ab[...] = total(recv_ab, 32)

    @pl.when(owns_b)
    def _():
        drain(recv_ab.at[pl.ds(0, 15)], rs_recv.at[1])
        part_ab[...] = total(recv_ab, 16)


    @pl.when(owns_ab)
    def _():
        for copy in deep_copies(part_ab, deep_ab, 0):
            copy.start()

    drain(recv_c.at[pl.ds(0, 7)], rs_recv.at[2])
    part_c[...] = total(recv_c, 8)
    for m, copy in zip(DEPTH, deep_copies(part_c, deep_c, 1)):
        if m & Z3:
            pl.when(core == 0)(copy.start)
        else:
            copy.start()

    d_do(lambda copy: copy.start())

    def active(columns, zone):
        lo, hi = ZONES[zone][0] * 128, sum(ZONES[zone]) * 128
        keep = None
        for level in range(9):
            if STARTS[level] < hi and ENDS[level] > lo:
                limit = STARTS[level] + sizes_ref[level]
                inside = jnp.logical_and(
                    jnp.logical_and(columns >= STARTS[level], columns < ENDS[level]), columns < limit)
                keep = inside if keep is None else jnp.logical_or(keep, inside)
        lo, hi = KEEP[zone]
        return jnp.logical_and(keep, jnp.logical_and(columns >= lo, columns < hi))

    def rounded(values, columns, end, zone):
        keep = jnp.logical_and(active(columns, zone), columns < end)
        return jnp.where(keep, values, 0.0).astype(BF16)

    d_do(lambda copy: copy.wait_recv())
    for j in range(WIDE[3]):
        columns, end = column_of(3, core, j)
        value = mine[AT[3] + j]
        for n, mask in enumerate(LINE):
            if mask & Z0:
                bound = jnp.where(core == 0, ENDS[5], 0)
            else:
                bound = ENDS[6] if mask & X1 else ENDS[7]
            value = value + jnp.where(columns < bound, recv_d[n, j], 0.0)
        full[0, AT[3] + j] = rounded(value, columns, end, 3)

    def relay(zone, at):
        blocks = pl.ds(AT[zone], WIDE[zone])
        return remote(full.at[0, blocks], full.at[1, blocks], relay_send.at[at], relay_recv.at[at], sibling)

    relay(3, 3).start()

    loc_copy.wait()
    x_loc = jnp.concatenate([xl[:, 1024 * s : 1024 * s + 1024] for s in range(4)], axis=0)
    interior = jnp.dot(rhs16, x_loc, preferred_element_type=F32).astype(BF16)
    contract = (((1,), (1,)), ((), ()))
    acc = lax.dot_general(interior, x_loc, contract, preferred_element_type=F32)

    def product(zone, half):
        blocks = jnp.concatenate([full[half, AT[zone] + j] for j in range(WIDE[zone])], axis=1)
        return lax.dot_general(blocks, windows(zone, half), contract, preferred_element_type=F32)

    def deep_total(part, landing):
        value = part[...]
        for i in range(7):
            value = value + landing[i]
        return value

    def gather(block, masks, sem):
        for mask in masks:
            remote(full.at[0, block], full.at[0, block], ag_send.at[sem], ag_recv.at[0, sem], partner(mask)).start()
            remote(full.at[0, block], full.at[1, block], ag_send.at[sem], ag_recv.at[1, sem], partner(mask | CORE)).start()
        remote(full.at[0, block], full.at[1, block], ag_send.at[sem], ag_recv.at[1, sem], partner(CORE)).start()

    @pl.when(owns_ab)
    def _():
        drain(deep_ab, z_recv.at[0])

    @pl.when(owns_a)
    def _():
        columns, end = column_of(0, core, a_mine)
        full[0, a_mine] = rounded(deep_total(part_ab, deep_ab), columns, end, 0)
        gather(a_mine, PLANE, 0)

    @pl.when(owns_b)
    def _():
        columns, end = column_of(1, core, k)
        full[0, AT[1] + k] = rounded(deep_total(part_ab, deep_ab), columns, end, 1)
        gather(AT[1] + k, PAIR, 1)

    @pl.when(core == 0)
    def _():
        drain(deep_c, z_recv.at[1])

    @pl.when(core == 1)
    def _():
        drain(deep_c.at[pl.ds(0, 3)], z_recv.at[1])

    columns, end = column_of(2, core, k)
    value = part_c[...]
    for m in range(1, 8):
        bound = ENDS[4] if m == 1 else ENDS[3] if m < 4 else jnp.where(core == 0, ENDS[2], 0)
        value = value + jnp.where(columns < bound, deep_c[m - 1], 0.0)
    full[0, AT[2] + k] = rounded(value, columns, end, 2)
    gather(AT[2] + k, LINE, 2)

    acc = acc + product(3, 0)
    relay(3, 3).wait_recv()
    acc = acc + product(3, 1)

    for zone in range(4):
        core_copies[zone].wait_send()
    relay(3, 3).wait_send()

    def drain_scatter(owns, zone):
        @pl.when(owns)
        def _():
            drain(mine.at[pl.ds(0, WIDE[zone] - 1)], rs_send.at[zone])

        @pl.when(jnp.logical_not(owns))
        def _():
            drain(mine.at[pl.ds(0, WIDE[zone])], rs_send.at[zone])

    drain_scatter(owns_a, 0)
    drain_scatter(owns_b, 1)
    drain(mine.at[pl.ds(0, 7)], rs_send.at[2])
    d_do(lambda copy: copy.wait_send())

    @pl.when(owns_ab)
    def _():
        drain(deep_ab, z_send.at[0])

    @pl.when(core == 0)
    def _():
        drain(deep_c, z_send.at[1])

    @pl.when(core == 1)
    def _():
        drain(deep_c.at[pl.ds(0, 3)], z_send.at[1])

    def drain_gather(owns, zone):
        if owns is None:
            drain(full.at[0, pl.ds(AT[zone], WIDE[zone] - 1)], ag_recv.at[0, zone])
            return

        @pl.when(owns)
        def _():
            drain(full.at[0, pl.ds(AT[zone], WIDE[zone] - 1)], ag_recv.at[0, zone])

        @pl.when(jnp.logical_not(owns))
        def _():
            drain(full.at[0, pl.ds(AT[zone], WIDE[zone])], ag_recv.at[0, zone])

    def arrived(owns, zone):
        drain_gather(owns, zone)
        drain(full.at[1, pl.ds(AT[zone], WIDE[zone])], ag_recv.at[1, zone])
        return product(zone, 0) + product(zone, 1)

    acc = acc + arrived(owns_b, 1)
    acc = acc + arrived(owns_a, 0)
    acc = acc + arrived(None, 2)
    out_ref[...] = (acc[0:4, 0:32] + acc[4:8, 32:64]) + (acc[8:12, 64:96] + acc[12:16, 96:128])

    @pl.when(owns_a)
    def _():
        drain(full, ag_send.at[0])
        drain(full.at[0, pl.ds(0, 1)], ag_send.at[0])

    @pl.when(owns_b)
    def _():
        drain(full.at[0, pl.ds(0, 31)], ag_send.at[1])

    drain(full.at[0, pl.ds(0, 15)], ag_send.at[2])


def body(rhs, x_sep, x_loc, sep_sizes):
    vmem, hbm = pl.BlockSpec(memory_space=pltpu.VMEM), pl.BlockSpec(memory_space=pltpu.HBM)
    dma = pltpu.SemaphoreType.DMA
    blocks = functools.partial(pltpu.VMEM, dtype=F32)
    return pl.pallas_call(
        kernel,
        out_shape=pltpu.VMEM((4, 32), F32),
        in_specs=[hbm] * 4,
        out_specs=vmem,
        scratch_shapes=[
            pltpu.VMEM((4, 32), BF16),
            pltpu.SMEM((9,), jnp.int32),
            pltpu.VMEM((2, 32, TILES * 128), BF16),
            pltpu.VMEM((32, COLS % 128), BF16),
            pltpu.VMEM((32, LOC), BF16),
            blocks((BLOCKS, 16, 128)),
            blocks((BLOCKS, 16, 128)),
            blocks((BLOCKS, 16, 128)),
            blocks((32, 16, 128)),
            blocks((8, 16, 128)),
            blocks((7, WIDE[3], 16, 128)),
            blocks((16, 128)),
            blocks((16, 128)),
            blocks((7, 16, 128)),
            blocks((7, 16, 128)),
            pltpu.VMEM((2, BLOCKS, 16, 128), BF16),
            dma((2,)),
            dma((2, 5)),
            dma,
            dma((4,)),
            dma((4,)),
            dma((10,)),
            dma((10,)),
            dma((2,)),
            dma((2,)),
            dma((3,)),
            dma((2, 3)),
            dma((4,)),
            dma((4,)),
            pltpu.SemaphoreType.REGULAR,
            pltpu.SemaphoreType.REGULAR,
        ],
        compiler_params=pltpu.CompilerParams(
            collective_id=0, has_side_effects=True, vmem_limit_bytes=60 * 1024 * 1024
        ),
        name="xxt",
    )(rhs, sep_sizes, x_sep, x_loc)


def solution(mesh):
    placed = (P(None, "leaf"), P("leaf", None), P("leaf", None), P())
    return jax.shard_map(
        body, mesh=mesh, in_specs=placed, out_specs=P(None, "leaf"), check_vma=False
    )
```
